128 devices in a mesh: rep: 16 (over z, x_lo, core), ctx: 4 (over y), tensor: 2 (over x_hi).
Axes of the slice: x: 4 (x_hi: 2, x_lo: 2; x = x_hi * 2 + x_lo), y: 4, z: 4, core: 2. Of those that a mesh axis runs over, the one named last changes fastest.
Arguments:
- tokens: bfloat16 [16, 1024, 1152], P('rep', 'ctx'), may hold values from -6 to 6
- doc_ids: int32 [16, 1024], P('rep'), may hold values from 0 to 2, as said below
- w_query: bfloat16 [1152, 1024], P('ctx', 'tensor'), may hold values from -0.1875 to 0.1875
- w_key: bfloat16 [1152, 256], P('ctx'), may hold values from -0.1875 to 0.1875
- w_value: bfloat16 [1152, 256], P('ctx'), may hold values from -0.1875 to 0.1875
- w_out: bfloat16 [1024, 1152], P('tensor', 'ctx'), may hold values from -0.1875 to 0.1875
- w_gate: bfloat16 [1152, 6912], P('ctx', 'tensor'), may hold values from -0.1875 to 0.1875
- w_up: bfloat16 [1152, 6912], P('ctx', 'tensor'), may hold values from -0.1875 to 0.1875
- w_down: bfloat16 [6912, 1152], P('tensor', 'ctx'), may hold values from -0.078125 to 0.078125
- gain_in: bfloat16 [1152], P('ctx'), may hold values from 0.5 to 1.5
- gain_attn_out: bfloat16 [1152], P('ctx'), may hold values from 0.5 to 1.5
- gain_query: bfloat16 [256], P('ctx'), may hold values from 0.5 to 1.5
- gain_key: bfloat16 [256], P('ctx'), may hold values from 0.5 to 1.5
- gain_ffn_in: bfloat16 [1152], P('ctx'), may hold values from 0.5 to 1.5
- gain_ffn_out: bfloat16 [1152], P('ctx'), may hold values from 0.5 to 1.5
- cotangent: bfloat16 [16, 1024, 1152], P('rep', 'ctx'), may hold values from -6 to 6
Outputs:
- layer_out: bfloat16 [16, 1024, 1152], P('rep', 'ctx')
- grad_tokens: float32 [16, 1024, 1152], P('rep', 'ctx')
- grad_w_query: float32 [1152, 1024], P('ctx', 'tensor')
- grad_w_key: float32 [1152, 256], P('ctx')
- grad_w_value: float32 [1152, 256], P('ctx')
- grad_w_out: float32 [1024, 1152], P('tensor', 'ctx')
- grad_w_gate: float32 [1152, 6912], P('ctx', 'tensor')
- grad_w_up: float32 [1152, 6912], P('ctx', 'tensor')
- grad_w_down: float32 [6912, 1152], P('tensor', 'ctx')
- grad_gain_in: float32 [1152], P('ctx')
- grad_gain_attn_out: float32 [1152], P('ctx')
- grad_gain_query: float32 [256], P('ctx')
- grad_gain_key: float32 [256], P('ctx')
- grad_gain_ffn_in: float32 [1152], P('ctx')
- grad_gain_ffn_out: float32 [1152], P('ctx')
The draws below stay inside these ranges and needn't reach their ends.
Inputs may be any that keep to these rules, and one draw needn't show every extreme that they name: `doc_ids`: in each pack the numbers never fall and take the values 0, 1 and 2: document 1 begins before position 128 and ends after position 895, documents 0 and 2 are the tokens before and after it.
All inputs are finite; a program needn't handle non-finite values.
Results may differ from the reference program's by a relative error of at most 0.029.
Values may be sent and summed in bfloat16 or wider, within the bound.
No kernel may reach another device: no remote copies, remote signals or barrier semaphores. Data moves between devices by JAX's collectives and lax.ppermute only.
A program may use at most 192 MiB of HBM per device.

```python
import jax
import jax.numpy as jnp
from jax import lax

D = 1152
HQ = 4
HD = 256
FF = 6912
WINDOW = 512
BLOCK = 256
PACKS = 16
LEN = 1024


def draw_doc_ids(key, part):
    key = jax.random.fold_in(key, 11)
    front_key, back_key = jax.random.split(key)
    margin = max(BLOCK // 2, 2)
    first_end = jax.random.randint(front_key, (PACKS, 1), 1, margin)
    second_end = LEN - jax.random.randint(back_key, (PACKS, 1), 1, margin)
    places = jnp.arange(LEN, dtype=jnp.int32)[None, :]
    return (places >= first_end).astype(jnp.int32) + (places >= second_end).astype(jnp.int32)


def level_of(own_key, shape, cuts, least, high):
    def one(dim, blocks):
        heights = jax.random.uniform(jax.random.fold_in(jax.random.fold_in(own_key, 6), dim), (blocks,), jnp.float32, least / len(cuts), high / len(cuts))
        return jnp.repeat(jnp.exp(heights), shape[dim] // blocks).reshape((-1,) + (1,) * (len(shape) - dim - 1))

    loudness = one(*cuts[0])
    for cut in cuts[1:]:
        loudness = loudness * one(*cut)
    return loudness


def normal_values(key, shape, deviation, most, shards=(), kind=jnp.bfloat16):
    loudness = level_of(key, shape, shards, -0.22, 0.18) if shards else 1.0
    drawn = jax.random.normal(key, shape, jnp.float32) * deviation * loudness
    return jnp.minimum(jnp.maximum(drawn, -most), most).astype(kind)


def setup_inputs(seed: int = 0) -> dict:
    key_of = jax.random.split(jax.random.key(seed), 17)
    tokens = normal_values(key_of[0], (PACKS, LEN, D), 1.0, 6.0, ((0, 16), (1, 4)))
    doc_ids = draw_doc_ids(jax.random.fold_in(key_of[16], 71), 0)
    w_query = normal_values(key_of[2], (D, HQ * HD), D ** -0.5, 0.1875, ((0, 4), (1, 2)))
    w_key = normal_values(key_of[3], (D, HD), D ** -0.5, 0.1875, ((0, 4),))
    w_value = normal_values(key_of[4], (D, HD), D ** -0.5, 0.1875, ((0, 4),))
    w_out = normal_values(key_of[5], (HQ * HD, D), (HQ * HD) ** -0.5, 0.1875, ((0, 2), (1, 4)))
    w_gate = normal_values(key_of[6], (D, FF), D ** -0.5, 0.1875, ((0, 4), (1, 2)))
    w_up = normal_values(key_of[7], (D, FF), D ** -0.5, 0.1875, ((0, 4), (1, 2)))
    w_down = normal_values(key_of[8], (FF, D), FF ** -0.5, 0.078125, ((0, 2), (1, 4)))
    gain_in = jnp.clip(1.0 + 0.1 * jax.random.normal(key_of[9], (D,), jnp.float32), 0.5, 1.5).astype(jnp.bfloat16)
    gain_attn_out = jnp.clip(1.0 + 0.1 * jax.random.normal(key_of[10], (D,), jnp.float32), 0.5, 1.5).astype(jnp.bfloat16)
    gain_query = jnp.clip(1.0 + 0.1 * jax.random.normal(key_of[11], (HD,), jnp.float32), 0.5, 1.5).astype(jnp.bfloat16)
    gain_key = jnp.clip(1.0 + 0.1 * jax.random.normal(key_of[12], (HD,), jnp.float32), 0.5, 1.5).astype(jnp.bfloat16)
    gain_ffn_in = jnp.clip(1.0 + 0.1 * jax.random.normal(key_of[13], (D,), jnp.float32), 0.5, 1.5).astype(jnp.bfloat16)
    gain_ffn_out = jnp.clip(1.0 + 0.1 * jax.random.normal(key_of[14], (D,), jnp.float32), 0.5, 1.5).astype(jnp.bfloat16)
    cotangent = normal_values(key_of[15], (PACKS, LEN, D), 1.0, 6.0, ((0, 16), (1, 4)))
    return dict(tokens=tokens, doc_ids=doc_ids, w_query=w_query, w_key=w_key, w_value=w_value, w_out=w_out, w_gate=w_gate, w_up=w_up, w_down=w_down, gain_in=gain_in, gain_attn_out=gain_attn_out, gain_query=gain_query, gain_key=gain_key, gain_ffn_in=gain_ffn_in, gain_ffn_out=gain_ffn_out, cotangent=cotangent)


EPSILON = 1e-06
ROTARY_BASE = 10000.0
MASKED = -1e+30
HIGHEST = lax.Precision.HIGHEST

@jax.custom_vjp
def low(v):
    return lax.optimization_barrier(v.astype(jnp.bfloat16)).astype(jnp.float32)

@jax.custom_vjp
def low_back(v):
    return v

def low_keep(v):
    return (low(v), None)

def low_pass(kept, grad):
    return (grad,)

def back_keep(v):
    return (v, None)

def back_low(kept, grad):
    return (low(grad),)
low.defvjp(low_keep, low_pass)
low_back.defvjp(back_keep, back_low)

def product(left, right):
    return jnp.dot(left, right, precision=HIGHEST)

def rms_norm(values, gain):
    scale = lax.rsqrt(lax.optimization_barrier(jnp.mean(values * values, axis=-1, keepdims=True)) + EPSILON)
    return values * scale * gain

def rotate(values, cosine, sine):
    half = values.shape[-1] // 2
    first = values[..., :half]
    second = values[..., half:]
    return jnp.concatenate([first * cosine - second * sine, second * cosine + first * sine], axis=-1)

def attend(queries, keys, values, doc_row):
    length = keys.shape[0]
    rows = min(512, length)
    blocks = length // rows
    spots = jnp.arange(length, dtype=jnp.int32)

    def block_rows(item):
        query_block, block_docs, block_spots = item
        scores = low_back(jnp.einsum('rhd,kd->hrk', query_block, keys, precision=HIGHEST))
        allowed = (block_docs[:, None] == doc_row[None, :]) & (spots[None, :] <= block_spots[:, None]) & (block_spots[:, None] - spots[None, :] < WINDOW)
        scores = jnp.where(allowed[None], scores, MASKED)
        largest = lax.optimization_barrier(jnp.max(scores, axis=-1, keepdims=True))
        total_log = largest + jnp.log(lax.optimization_barrier(jnp.sum(jnp.exp(scores - largest), axis=-1, keepdims=True)))
        probs = jnp.exp(scores - total_log)
        return jnp.einsum('hrk,kd->rhd', low(probs), values, precision=HIGHEST)
    outputs = lax.map(jax.checkpoint(block_rows), (queries.reshape(blocks, rows, HQ, HD), doc_row.reshape(blocks, rows), spots.reshape(blocks, rows)))
    return outputs.reshape(length, HQ * HD)

def layer(inputs, w_query, w_key, w_value, w_out, w_gate, w_up, w_down, gain_in, gain_attn_out, gain_query, gain_key, gain_ffn_in, gain_ffn_out, doc_row):
    length = inputs.shape[0]
    spots = jnp.arange(length, dtype=jnp.int32)
    earlier = lax.optimization_barrier(jnp.sum((doc_row[None, :] < doc_row[:, None]).astype(jnp.int32), axis=1))
    places = (spots - earlier).astype(jnp.float32)
    half = HD // 2
    freqs = ROTARY_BASE ** (-2.0 * jnp.arange(half, dtype=jnp.float32) / HD)
    angles = places[:, None] * freqs[None, :]
    cosine = jnp.cos(angles)
    sine = jnp.sin(angles)
    normed = low(rms_norm(inputs, gain_in))
    query_raw = low_back(product(normed, w_query)).reshape(length, HQ, HD)
    key_raw = low_back(product(normed, w_key))
    values = low(low_back(product(normed, w_value)))
    queries = low(rotate(rms_norm(query_raw, gain_query), cosine[:, None, :], sine[:, None, :]) * HD ** (-0.5))
    keys = low(rotate(rms_norm(key_raw, gain_key), cosine, sine))
    attended = low(low_back(attend(queries, keys, values, doc_row)))
    branch = low_back(product(attended, w_out))
    hidden = inputs + rms_norm(branch, gain_attn_out)
    ffn_in = low(rms_norm(hidden, gain_ffn_in))
    gate = low_back(product(ffn_in, w_gate))
    upward = low_back(product(ffn_in, w_up))
    active = low(jax.nn.gelu(gate, approximate=True) * upward)
    result = low_back(product(active, w_down))
    return hidden + rms_norm(result, gain_ffn_out)

def reference(tokens, doc_ids, w_query, w_key, w_value, w_out, w_gate, w_up, w_down, gain_in, gain_attn_out, gain_query, gain_key, gain_ffn_in, gain_ffn_out, cotangent):
    weights = (w_query, w_key, w_value, w_out, w_gate, w_up, w_down, gain_in, gain_attn_out, gain_query, gain_key, gain_ffn_in, gain_ffn_out)
    weights = tuple((item.astype(jnp.float32) for item in weights))

    def one_pack(totals, item):
        pack_tokens, pack_docs, pack_cotangent = item

        def forward(inputs, params):
            return layer(inputs, params[0], params[1], params[2], params[3], params[4], params[5], params[6], params[7], params[8], params[9], params[10], params[11], params[12], pack_docs)
        output, pull = jax.vjp(forward, pack_tokens, weights)
        input_grad, param_grads = pull(pack_cotangent)
        totals = tuple((total + grad for total, grad in zip(totals, param_grads)))
        return (totals, (output.astype(jnp.bfloat16), input_grad))
    begin = tuple((jnp.zeros(item.shape, jnp.float32) for item in weights))
    totals, (outputs, token_grads) = lax.scan(one_pack, begin, (tokens.astype(jnp.float32), doc_ids, cotangent.astype(jnp.float32)))
    return (outputs, token_grads, totals[0], totals[1], totals[2], totals[3], totals[4], totals[5], totals[6], totals[7], totals[8], totals[9], totals[10], totals[11], totals[12])
```

```python
import jax
import jax.numpy as jnp
from jax import lax
from jax.sharding import PartitionSpec as P

WINDOW = 512
EPSILON = 1e-06
ROTARY_BASE = 10000.0
MASKED = -1e30
LOW = jnp.bfloat16
WIDE = jnp.float32

RING = range(4)
REP = range(16)
ROUTES = {
    "y+": ("ctx", [(i, (i + 1) % 4) for i in RING]),
    "y-": ("ctx", [(i, (i - 1) % 4) for i in RING]),
    "z+": ("rep", [(i, (i + 4) % 16) for i in REP]),
    "z-": ("rep", [(i, (i - 4) % 16) for i in REP]),
    "x": ("rep", [(i, i ^ 2) for i in REP]),
    "core": ("rep", [(i, i ^ 1) for i in REP]),
    "tensor": ("tensor", [(0, 1), (1, 0)]),
    "later1": ("ctx", [(0, 1), (1, 2), (2, 3)]),
    "later2": ("ctx", [(0, 2), (1, 3)]),
    "earlier1": ("ctx", [(1, 0), (2, 1), (3, 2)]),
    "earlier2": ("ctx", [(2, 0), (3, 1)]),
}


def send(x, route):
    axis, pairs = ROUTES[route]
    return lax.ppermute(x, axis, pairs)


def middle(rows):
    return rows // 2 if rows < 16 else rows // 16 * 8


def ring_gather(x, axis):
    h = middle(x.shape[0])
    previous = send(x, axis + "+")
    following = send(x, axis + "-")
    opposite = jnp.concatenate(
        [send(previous[:h], axis + "+"), send(following[h:], axis + "-")], axis=0
    )
    return [x, following, opposite, previous]


def ring_scatter(blocks, axis):
    own, following, opposite, previous = blocks
    h = middle(own.shape[0])
    above = send(opposite[:h], axis + "+")
    below = send(opposite[h:], axis + "-")
    following = jnp.concatenate([add(following[:h], above), following[h:]], axis=0)
    previous = jnp.concatenate([previous[:h], add(previous[h:], below)], axis=0)
    from_previous = send(following, axis + "+")
    from_following = send(previous, axis + "-")
    total = own.astype(WIDE) + from_previous.astype(WIDE) + from_following.astype(WIDE)
    return total.astype(LOW)


def add(a, b):
    return (a.astype(WIDE) + b.astype(WIDE)).astype(LOW)


def relative(x, at, dim):
    return [
        lax.dynamic_index_in_dim(x, lax.rem(at + j, 4), dim, keepdims=False) for j in RING
    ]


def absolute(blocks, at, dim):
    whole = jnp.zeros(
        blocks[0].shape[:dim] + (4,) + blocks[0].shape[dim:], blocks[0].dtype
    )
    for j, block in enumerate(blocks):
        whole = lax.dynamic_update_index_in_dim(whole, block, lax.rem(at + j, 4), dim)
    return whole


def turned(x, steps, width):
    out = x
    for j in (1, 2, 3):
        out = jnp.where(steps == j, jnp.roll(x, -j * width, axis=-1), out)
    return out


def rms_norm(values, gain):
    scale = lax.rsqrt(jnp.mean(values * values, axis=-1, keepdims=True) + EPSILON)
    return values * scale * gain


def rotate(values, cosine, sine):
    half = values.shape[-1] // 2
    first = values[..., :half]
    second = values[..., half:]
    return jnp.concatenate(
        [first * cosine - second * sine, second * cosine + first * sine], axis=-1
    )


def dot_plain(left, right):
    return jnp.dot(left, right, preferred_element_type=WIDE)


def dot_right(left, right):
    return lax.dot_general(left, right, (((1,), (1,)), ((), ())), preferred_element_type=WIDE)


def dot_left(left, right):
    return lax.dot_general(left, right, (((0,), (0,)), ((), ())), preferred_element_type=WIDE)


def over_tensor(part):
    mine = part.astype(LOW)
    return mine.astype(WIDE) + send(mine, "tensor").astype(WIDE)


def with_core(x):
    return jnp.concatenate([x, send(x, "core")], axis=0)


def for_own(part, span):
    return part[:span] + send(part[span:].astype(LOW), "core").astype(WIDE)


def shards(
    tokens,
    doc_ids,
    w_query,
    w_key,
    w_value,
    w_out,
    w_gate,
    w_up,
    w_down,
    gain_in,
    gain_attn_out,
    gain_query,
    gain_key,
    gain_ffn_in,
    gain_ffn_out,
    cotangent,
):
    c = lax.axis_index("ctx")
    rep = lax.axis_index("rep")
    z = rep // 4
    first_core = rep % 2 == 0
    width = w_query.shape[0]
    model = 4 * width
    head_size = w_key.shape[1]
    heads = w_query.shape[1] // head_size
    hidden_half = w_gate.shape[1] // 2
    zrows = width // 4
    span = tokens.shape[1]

    gains = jnp.concatenate(
        [gain_in, gain_attn_out, gain_ffn_in, gain_ffn_out, gain_query, gain_key]
    )
    gain_rows = jnp.pad(gains, (0, 8 * 512 - gains.shape[0])).reshape(8, 512)
    w_out_t = w_out.T
    w_kv = jnp.concatenate([w_key, w_value], axis=1)
    half_out = width // 2
    attn_own = jnp.concatenate(
        [
            jnp.where(first_core, w_query, w_kv),
            jnp.where(first_core, w_out_t[:half_out], w_out_t[half_out:]),
            gain_rows,
        ],
        axis=0,
    )
    attn_blocks = ring_gather(attn_own, "y")
    attn_stack = jnp.stack(attn_blocks)
    swap_rows = width + half_out
    mine = attn_stack[:, :swap_rows]
    theirs = send(mine, "core")
    low_half = jnp.where(first_core, mine, theirs)
    high_half = jnp.where(first_core, theirs, mine)
    full_query = low_half[:, :width].reshape(model, -1)
    full_kv = high_half[:, :width].reshape(model, -1)
    full_out_t = jnp.concatenate([low_half[:, width:], high_half[:, width:]], axis=1).reshape(
        model, -1
    )
    gain_table = attn_stack[:, swap_rows:].reshape(4, -1).astype(WIDE)
    norm_in, norm_attn, norm_ffn_in, norm_ffn_out = (
        gain_table[:, k * width : (k + 1) * width].reshape(model) for k in range(4)
    )
    head_gains = gain_table[:, 4 * width : 4 * width + head_size // 2]
    head_gains = lax.dynamic_slice_in_dim(
        jnp.concatenate([head_gains, head_gains], axis=0), lax.rem(4 - c, 4), 4
    )
    norm_query = head_gains[:, : head_size // 4].reshape(head_size)
    norm_key = head_gains[:, head_size // 4 :].reshape(head_size)

    def core_half(x):
        return jnp.where(first_core, x[:, :hidden_half], x[:, hidden_half:])

    gate_own = core_half(w_gate)
    up_own = core_half(w_up)
    down_own = core_half(w_down.T)
    full_gate = jnp.concatenate(ring_gather(gate_own, "y"), axis=0)
    pair_own = jnp.stack([up_own, down_own])
    pair_part = lax.dynamic_slice_in_dim(pair_own, z * zrows, zrows, axis=1)
    pair_rest = jnp.stack(ring_gather(pair_part, "y")[1:], axis=1)
    pair_rest = absolute(ring_gather(pair_rest, "z"), z, 2)
    pair = jnp.concatenate(
        [pair_own, pair_rest.reshape(2, 3 * width, hidden_half)], axis=1
    )
    full_up = pair[0]
    full_down_t = pair[1]

    inputs = turned(tokens[0], c, width).astype(WIDE)
    outward = turned(cotangent[0], c, width).astype(WIDE)
    start = c * span
    doc_row = doc_ids[0]
    reach = 2 * span
    query_docs = lax.dynamic_slice_in_dim(doc_row, start, span)
    query_at = start + jnp.arange(span, dtype=jnp.int32)
    earlier = jnp.sum((doc_row[None, :] < query_docs[:, None]).astype(jnp.int32), axis=1)
    places = (query_at - earlier).astype(WIDE)
    half = head_size // 2
    freqs = ROTARY_BASE ** (-2.0 * jnp.arange(half, dtype=WIDE) / head_size)
    angles = places[:, None] * freqs[None, :]
    cosine = jnp.cos(angles)
    sine = jnp.sin(angles)
    padded_docs = jnp.concatenate([jnp.full((reach,), -1, jnp.int32), doc_row])
    key_docs = lax.dynamic_slice_in_dim(padded_docs, start, reach + span)
    key_at = start - reach + jnp.arange(reach + span, dtype=jnp.int32)
    allowed = (
        (query_docs[:, None] == key_docs[None, :])
        & (key_at[None, :] <= query_at[:, None])
        & (query_at[:, None] - key_at[None, :] < WINDOW)
    )

    def query_prep(raw, gain):
        return rotate(rms_norm(raw, gain), cosine[:, None, :], sine[:, None, :]) * head_size ** (
            -0.5
        )

    def key_prep(raw, gain):
        return rotate(rms_norm(raw, gain), cosine, sine)

    normed_low = rms_norm(inputs, norm_in).astype(LOW)
    kv_raw = dot_plain(normed_low, full_kv)
    key_raw = kv_raw[:, :head_size]
    key_low = key_prep(key_raw, norm_key).astype(LOW)
    value_low = kv_raw[:, head_size:].astype(LOW)
    kv_low = jnp.concatenate([key_low, value_low], axis=1)
    all_kv = jnp.concatenate([send(kv_low, "later2"), send(kv_low, "later1"), kv_low], axis=0)
    all_keys = all_kv[:, :head_size]
    all_values = all_kv[:, head_size:]
    query_raw = dot_plain(normed_low, full_query).reshape(span, heads, head_size)
    query_low = query_prep(query_raw, norm_query).astype(LOW)
    raw = jnp.einsum("chd,kd->hck", query_low, all_keys, preferred_element_type=WIDE)
    scores = jnp.where(allowed[None], raw, MASKED)
    largest = jnp.max(scores, axis=-1, keepdims=True)
    total_log = largest + jnp.log(jnp.sum(jnp.exp(scores - largest), axis=-1, keepdims=True))
    probs = jnp.exp(scores - total_log)
    probs_low = probs.astype(LOW)
    attended = jnp.einsum("hck,kd->chd", probs_low, all_values, preferred_element_type=WIDE)
    attended_low = attended.reshape(span, heads * head_size).astype(LOW)
    branch = over_tensor(dot_right(attended_low, full_out_t))
    hidden = inputs + rms_norm(branch, norm_attn)

    ffn_in_low = rms_norm(hidden, norm_ffn_in).astype(LOW)
    ffn_rows = with_core(ffn_in_low)
    gate = dot_plain(ffn_rows, full_gate)
    upward = dot_plain(ffn_rows, full_up)
    active_low = (jax.nn.gelu(gate, approximate=True) * upward).astype(LOW)
    result = over_tensor(for_own(dot_right(active_low, full_down_t), span))
    output = hidden + rms_norm(result, norm_ffn_out)
    unused, pull_out = jax.vjp(rms_norm, result, norm_ffn_out)
    grad_result, grad_gain_ffn_out = pull_out(outward)
    result_rows = with_core(grad_result.astype(LOW))
    grad_active = dot_plain(result_rows, full_down_t)

    def geglu(left, right):
        return jax.nn.gelu(left, approximate=True) * right

    unused, pull_geglu = jax.vjp(geglu, gate, upward)
    grad_gate, grad_upward = pull_geglu(grad_active)
    gate_low = grad_gate.astype(LOW)
    upward_low = grad_upward.astype(LOW)
    grad_ffn_in = over_tensor(
        for_own(dot_right(gate_low, full_gate) + dot_right(upward_low, full_up), span)
    )
    unused, pull_ffn_norm = jax.vjp(rms_norm, hidden, norm_ffn_in)
    grad_hidden_norm, grad_gain_ffn_in = pull_ffn_norm(grad_ffn_in)
    grad_hidden = outward + grad_hidden_norm

    down_part = dot_left(result_rows, active_low).astype(LOW)
    down_sum = ring_scatter([down_part[j * width : (j + 1) * width] for j in RING], "y")
    down_sum = ring_scatter(relative(down_sum.reshape(4, zrows, hidden_half), z, 0), "z")
    down_sum = add(down_sum, send(down_sum, "x"))
    down_sum = absolute(ring_gather(down_sum, "z"), z, 0).reshape(width, hidden_half)

    pair_part = jnp.stack(
        [dot_left(ffn_rows, gate_low).astype(LOW), dot_left(ffn_rows, upward_low).astype(LOW)]
    ).reshape(2, 4, 4, zrows, hidden_half)
    pair_sum = ring_scatter(relative(pair_part, z, 2), "z")
    pair_sum = ring_scatter([pair_sum[:, j] for j in RING], "y")
    pair_sum = add(pair_sum, send(pair_sum, "x"))
    pair_sum = absolute(ring_gather(pair_sum, "z"), z, 1).reshape(2, width, hidden_half)

    def both_cores(x):
        other = send(x, "core")
        return jnp.concatenate(
            [jnp.where(first_core, x, other), jnp.where(first_core, other, x)], axis=-1
        ).astype(WIDE)

    grad_w_down = both_cores(down_sum).T
    pair_both = both_cores(pair_sum)
    grad_w_gate = pair_both[0]
    grad_w_up = pair_both[1]

    unused, pull_attn_norm = jax.vjp(rms_norm, branch, norm_attn)
    grad_branch, grad_gain_attn_out = pull_attn_norm(grad_hidden)
    branch_low = grad_branch.astype(LOW)
    grad_attended = dot_plain(branch_low, full_out_t).reshape(span, heads, head_size).astype(LOW)
    grad_probs = jnp.einsum(
        "chd,kd->hck", grad_attended, all_values, preferred_element_type=WIDE
    )
    grad_scores = (
        probs * (grad_probs - jnp.sum(probs * grad_probs, axis=-1, keepdims=True))
    ).astype(LOW)
    grad_queries = jnp.einsum("hck,kd->chd", grad_scores, all_keys, preferred_element_type=WIDE)
    grad_keys = jnp.einsum("hck,chd->kd", grad_scores, query_low, preferred_element_type=WIDE)
    grad_values = jnp.einsum(
        "hck,chd->kd", probs_low, grad_attended, preferred_element_type=WIDE
    )
    grad_kv = jnp.concatenate([grad_keys, grad_values], axis=1)
    grad_kv_low = grad_kv[:reach].astype(LOW)
    own_kv = (
        grad_kv[reach:]
        + send(grad_kv_low[span:], "earlier1").astype(WIDE)
        + send(grad_kv_low[:span], "earlier2").astype(WIDE)
    )
    unused, pull_query = jax.vjp(query_prep, query_raw, norm_query)
    grad_query_raw, grad_gain_query = pull_query(grad_queries)
    query_grad_low = grad_query_raw.reshape(span, heads * head_size).astype(LOW)
    unused, pull_key = jax.vjp(key_prep, key_raw, norm_key)
    grad_key_raw, grad_gain_key = pull_key(own_kv[:, :head_size])
    kv_grad_low = jnp.concatenate([grad_key_raw, own_kv[:, head_size:]], axis=1).astype(LOW)
    normed_part = dot_right(query_grad_low, full_query) + dot_right(kv_grad_low, full_kv)
    unused, pull_gain = jax.vjp(lambda gain: rms_norm(inputs, gain), norm_in)
    (grad_gain_in,) = pull_gain(normed_part)
    grad_normed = over_tensor(normed_part)
    unused, pull_in = jax.vjp(lambda v: rms_norm(v, norm_in), inputs)
    (grad_inputs_norm,) = pull_in(grad_normed)
    grad_inputs = grad_hidden + grad_inputs_norm

    own_terms = jnp.concatenate(
        [
            dot_left(normed_low, query_grad_low).astype(LOW).reshape(4, width, -1),
            dot_left(branch_low, attended_low).astype(LOW).reshape(4, width, -1),
        ],
        axis=1,
    )
    head_grads = jnp.concatenate(
        [grad_gain_query.reshape(4, -1), grad_gain_key.reshape(4, -1)], axis=1
    )
    head_grads = lax.dynamic_slice_in_dim(
        jnp.concatenate([head_grads, head_grads], axis=0), c, 4
    )
    gain_terms = jnp.concatenate(
        [
            grad_gain_in.reshape(4, width),
            0.5 * grad_gain_attn_out.reshape(4, width),
            0.5 * grad_gain_ffn_in.reshape(4, width),
            0.5 * grad_gain_ffn_out.reshape(4, width),
            head_grads,
        ],
        axis=1,
    ).astype(LOW)
    gain_terms = jnp.pad(gain_terms, ((0, 0), (0, 32 * 512 - gain_terms.shape[1])))
    shared_terms = jnp.concatenate(
        [
            dot_left(normed_low, kv_grad_low).astype(LOW).reshape(4, width, -1),
            gain_terms.reshape(4, 32, 512),
        ],
        axis=1,
    )
    terms = jnp.concatenate(
        [own_terms.reshape(4, 2, 4, -1, 512), shared_terms.reshape(4, 2, 4, -1, 512)], axis=3
    )
    split = own_terms.shape[1] // 8
    kept = jnp.where(first_core, terms[:, 0], terms[:, 1])
    given = jnp.where(first_core, terms[:, 1], terms[:, 0])
    attn_sum = add(kept, send(given, "core"))
    attn_sum = ring_scatter([attn_sum[j] for j in RING], "y")
    attn_sum = ring_scatter(relative(attn_sum, z, 0), "z")
    attn_sum = add(attn_sum, send(attn_sum, "x"))
    shared = attn_sum[split:]
    attn_sum = jnp.concatenate([attn_sum[:split], add(shared, send(shared, "tensor"))], axis=0)
    attn_sum = absolute(ring_gather(attn_sum, "z"), z, 0)
    other_sum = send(attn_sum, "core")
    attn_sum = jnp.stack(
        [
            jnp.where(first_core, attn_sum, other_sum),
            jnp.where(first_core, other_sum, attn_sum),
        ]
    ).astype(WIDE)
    own_sums = attn_sum[:, :, :split].reshape(2 * width, 512)
    shared_sums = attn_sum[:, :, split:].reshape(width + 32, 512)
    gain_sums = shared_sums[width:].reshape(-1)
    gain_outs = [gain_sums[k * width : (k + 1) * width] for k in range(4)]
    head_outs = gain_sums[4 * width : 4 * width + head_size // 2]

    return (
        turned(output.astype(LOW), (4 - c) % 4, width)[None],
        turned(grad_inputs, (4 - c) % 4, width)[None],
        own_sums[:width],
        shared_sums[:width, :head_size],
        shared_sums[:width, head_size:],
        own_sums[width:].T,
        grad_w_gate,
        grad_w_up,
        grad_w_down,
        gain_outs[0],
        gain_outs[1],
        head_outs[: head_size // 4],
        head_outs[head_size // 4 :],
        gain_outs[2],
        gain_outs[3],
    )


def solution(mesh):
    return jax.shard_map(
        shards,
        mesh=mesh,
        in_specs=(
            P("rep", "ctx", None),
            P("rep", None),
            P("ctx", "tensor"),
            P("ctx", None),
            P("ctx", None),
            P("tensor", "ctx"),
            P("ctx", "tensor"),
            P("ctx", "tensor"),
            P("tensor", "ctx"),
            P("ctx"),
            P("ctx"),
            P("ctx"),
            P("ctx"),
            P("ctx"),
            P("ctx"),
            P("rep", "ctx", None),
        ),
        out_specs=(
            P("rep", "ctx", None),
            P("rep", "ctx", None),
            P("ctx", "tensor"),
            P("ctx", None),
            P("ctx", None),
            P("tensor", "ctx"),
            P("ctx", "tensor"),
            P("ctx", "tensor"),
            P("tensor", "ctx"),
            P("ctx"),
            P("ctx"),
            P("ctx"),
            P("ctx"),
            P("ctx"),
            P("ctx"),
        ),
        check_vma=False,
    )
```

```python
import jax
import jax.numpy as jnp
from jax import lax
from jax.sharding import Mesh
from jax.sharding import PartitionSpec as P

WINDOW = 512
EPSILON = 1e-06
ROTARY_BASE = 10000.0
MASKED = -1e30
GELU = 0.7978845608028654
LOW = jnp.bfloat16
WIDE = jnp.float32

RING = [(i, (i + 1) % 4) for i in range(4)]
BACK = [(i, (i - 1) % 4) for i in range(4)]
ACROSS = [(i, (i + 2) % 4) for i in range(4)]
SWAP = [(0, 1), (1, 0)]


def send(x, axis, pairs):
    return lax.ppermute(x, axis, pairs)


def swapped(x, axis):
    return lax.ppermute(x, axis, SWAP)


def after(x, *others):
    return lax.optimization_barrier((x, *others))[0]


def middle(rows):
    return rows // 2 if rows < 16 else rows // 16 * 8


def direct_gather(x, axis):
    previous = send(x, axis, RING)
    following = send(x, axis, BACK)
    opposite = send(x, axis, ACROSS)
    return [x, following, opposite, previous]


def ring_scatter(blocks, axis):
    own, following, opposite, previous = blocks
    h = middle(own.shape[0])
    above = send(opposite[:h], axis, RING)
    below = send(opposite[h:], axis, BACK)
    following = jnp.concatenate([add(following[:h], above), following[h:]], axis=0)
    previous = jnp.concatenate([previous[:h], add(previous[h:], below)], axis=0)
    from_previous = send(following, axis, RING)
    from_following = send(previous, axis, BACK)
    total = own.astype(WIDE) + from_previous.astype(WIDE) + from_following.astype(WIDE)
    return total.astype(LOW)


def exchanged_sum(x, axis):
    moved = lax.all_to_all(x, axis, split_axis=0, concat_axis=0, tiled=True)
    return moved.astype(WIDE).sum(axis=0).astype(LOW)


def add(a, b):
    return (a.astype(WIDE) + b.astype(WIDE)).astype(LOW)


def absolute(blocks, at, dim):
    whole = jnp.zeros(
        blocks[0].shape[:dim] + (4,) + blocks[0].shape[dim:], blocks[0].dtype
    )
    for j, block in enumerate(blocks):
        whole = lax.dynamic_update_index_in_dim(whole, block, lax.rem(at + j, 4), dim)
    return whole


def rms_norm(values, gain):
    scale = lax.rsqrt(jnp.mean(values * values, axis=-1, keepdims=True) + EPSILON)
    return values * scale * gain


def rotate(values, cosine, sine):
    half = values.shape[-1] // 2
    first = values[..., :half]
    second = values[..., half:]
    return jnp.concatenate(
        [first * cosine - second * sine, second * cosine + first * sine], axis=-1
    )


def dot_plain(left, right):
    return jnp.dot(left, right, preferred_element_type=WIDE)


def dot_right(left, right):
    return lax.dot_general(left, right, (((1,), (1,)), ((), ())), preferred_element_type=WIDE)


def dot_left(left, right):
    return lax.dot_general(left, right, (((0,), (0,)), ((), ())), preferred_element_type=WIDE)


def with_core(x):
    return jnp.concatenate([x, swapped(x, "core")], axis=0)


def shards(
    tokens,
    doc_ids,
    w_query,
    w_key,
    w_value,
    w_out,
    w_gate,
    w_up,
    w_down,
    gain_in,
    gain_attn_out,
    gain_query,
    gain_key,
    gain_ffn_in,
    gain_ffn_out,
    cotangent,
):
    c = lax.axis_index("ctx")
    z = lax.axis_index("z")
    first_core = lax.axis_index("core") == 0
    width = w_query.shape[0]
    model = 4 * width
    head_size = w_key.shape[1]
    heads = w_query.shape[1] // head_size
    hidden_half = w_gate.shape[1] // 2
    zrows = width // 4
    span = tokens.shape[1]

    def gain_row(gain):
        return jnp.pad(gain, (0, 512 - gain.shape[-1]))[None]

    gain_rows = jnp.concatenate(
        [
            gain_row(gain)
            for gain in (gain_in, gain_attn_out, gain_ffn_in, gain_ffn_out, gain_query, gain_key)
        ]
        + [jnp.zeros((2, 512), LOW)],
        axis=0,
    )
    w_out_t = w_out.T
    w_kv = jnp.concatenate([w_key, w_value], axis=1)
    half_out = width // 2
    attn_own = jnp.concatenate(
        [
            jnp.where(first_core, w_query, w_kv),
            jnp.where(first_core, w_out_t[:half_out], w_out_t[half_out:]),
            gain_rows,
        ],
        axis=0,
    )
    attn_stack = absolute(direct_gather(attn_own, "ctx"), c, 0)
    swap_rows = width + half_out
    mine = attn_stack[:, :swap_rows]
    theirs = swapped(mine, "core")
    full_query = jnp.where(first_core, mine[:, :width], theirs[:, :width]).reshape(model, -1)
    full_kv = jnp.where(first_core, theirs[:, :width], mine[:, :width]).reshape(model, -1)
    full_out_t = jnp.concatenate(
        [
            jnp.where(first_core, mine[:, width:], theirs[:, width:]),
            jnp.where(first_core, theirs[:, width:], mine[:, width:]),
        ],
        axis=1,
    ).reshape(model, -1)
    gain_table = attn_stack[:, swap_rows:].astype(WIDE)
    norm_in, norm_attn, norm_ffn_in, norm_ffn_out = (
        gain_table[:, k, :width].reshape(model) for k in range(4)
    )
    norm_query, norm_key = (
        gain_table[:, k, : head_size // 4].reshape(head_size) for k in (4, 5)
    )

    def core_half(x):
        return jnp.where(first_core, x[:, :hidden_half], x[:, hidden_half:])

    full_gate = lax.all_gather(core_half(w_gate), "ctx", axis=0, tiled=True)
    pair_own = jnp.stack([core_half(w_up), core_half(w_down.T)])
    pair_part = lax.dynamic_slice_in_dim(pair_own, z * zrows, zrows, axis=1)
    pair_rest = jnp.stack(direct_gather(pair_part, "ctx")[1:], axis=1)

    inputs = tokens[0].astype(WIDE)
    outward = cotangent[0].astype(WIDE)
    start = c * span
    doc_row = doc_ids[0]
    reach = 2 * span
    query_docs = lax.dynamic_slice_in_dim(doc_row, start, span)
    query_at = start + jnp.arange(span, dtype=jnp.int32)
    earlier = jnp.sum((doc_row[None, :] < query_docs[:, None]).astype(jnp.int32), axis=1)
    places = (query_at - earlier).astype(WIDE)
    half = head_size // 2
    freqs = ROTARY_BASE ** (-2.0 * jnp.arange(half, dtype=WIDE) / head_size)
    angles = places[:, None] * freqs[None, :]
    cosine = jnp.cos(angles)
    sine = jnp.sin(angles)
    padded_docs = jnp.concatenate([jnp.full((reach,), -1, jnp.int32), doc_row])
    key_docs = lax.dynamic_slice_in_dim(padded_docs, start, reach + span)
    key_at = start - reach + jnp.arange(reach + span, dtype=jnp.int32)
    allowed = (
        (query_docs[:, None] == key_docs[None, :])
        & (key_at[None, :] <= query_at[:, None])
        & (query_at[:, None] - key_at[None, :] < WINDOW)
    )

    def query_prep(raw, gain):
        return rotate(rms_norm(raw, gain), cosine[:, None, :], sine[:, None, :]) * head_size ** (
            -0.5
        )

    def key_prep(raw, gain):
        return rotate(rms_norm(raw, gain), cosine, sine)

    normed_low = rms_norm(inputs, norm_in).astype(LOW)
    kv_raw = dot_plain(normed_low, full_kv)
    key_raw = kv_raw[:, :head_size]
    key_low = key_prep(key_raw, norm_key).astype(LOW)
    value_low = kv_raw[:, head_size:].astype(LOW)
    kv_low = jnp.concatenate([key_low, value_low], axis=1)
    before2 = send(kv_low, "ctx", [(0, 2), (1, 3)])
    before1 = send(kv_low, "ctx", [(0, 1), (1, 2), (2, 3)])
    pair_rest = after(pair_rest, kv_low)
    pair_previous = send(pair_rest, "z", RING)
    pair_following = send(pair_rest, "z", BACK)
    query_raw = dot_plain(normed_low, full_query).reshape(span, heads, head_size)
    query_low = query_prep(query_raw, norm_query).astype(LOW)
    all_kv = jnp.concatenate([before2, before1, kv_low], axis=0)
    all_keys = all_kv[:, :head_size]
    all_values = all_kv[:, head_size:]
    raw = jnp.einsum("chd,kd->hck", query_low, all_keys, preferred_element_type=WIDE)
    scores = jnp.where(allowed[None], raw, MASKED)
    largest = jnp.max(scores, axis=-1, keepdims=True)
    total_log = largest + jnp.log(jnp.sum(jnp.exp(scores - largest), axis=-1, keepdims=True))
    probs = jnp.exp(scores - total_log)
    probs_low = probs.astype(LOW)
    attended = jnp.einsum("hck,kd->chd", probs_low, all_values, preferred_element_type=WIDE)
    attended_low = attended.reshape(span, heads * head_size).astype(LOW)
    branch_mine = dot_right(attended_low, full_out_t).astype(LOW)
    branch_theirs = swapped(branch_mine, "tensor")
    pair_previous, pair_following = lax.optimization_barrier(
        (pair_previous, pair_following, branch_mine)
    )[:2]
    pair_opposite = jnp.concatenate(
        [send(pair_previous[:1], "z", RING), send(pair_following[1:], "z", BACK)], axis=0
    )
    branch = branch_mine.astype(WIDE) + branch_theirs.astype(WIDE)
    hidden = inputs + rms_norm(branch, norm_attn)

    ffn_in_low = rms_norm(hidden, norm_ffn_in).astype(LOW)
    ffn_rows = with_core(ffn_in_low)
    pair_rest = absolute([pair_rest, pair_following, pair_opposite, pair_previous], z, 2)
    pair_rest = pair_rest.reshape(2, 3, width, hidden_half)
    pair = absolute([pair_own] + [pair_rest[:, j] for j in range(3)], c, 1)
    full_up = pair[0].reshape(model, hidden_half)
    full_down_t = pair[1].reshape(model, hidden_half)
    gate = dot_plain(ffn_rows, full_gate)
    upward = dot_plain(ffn_rows, full_up)
    bend = GELU * (1.0 + 0.134145 * gate * gate)
    level = jnp.tanh(GELU * gate * (1.0 + 0.044715 * gate * gate))
    gelu = 0.5 * gate * (1.0 + level)
    gelu_slope = 0.5 * (1.0 + level) + 0.5 * gate * (1.0 - level * level) * bend
    active_low = (gelu * upward).astype(LOW)
    gelu_low = gelu.astype(LOW)
    gate_factor = (upward * gelu_slope).astype(LOW)
    result_part = dot_right(active_low, full_down_t)
    result_given = result_part[span:].astype(LOW)
    result_mine = (
        result_part[:span] + swapped(result_given, "core").astype(WIDE)
    ).astype(LOW)
    result = result_mine.astype(WIDE) + swapped(result_mine, "tensor").astype(WIDE)
    unused, pull_out = jax.vjp(rms_norm, result, norm_ffn_out)
    grad_result, grad_gain_ffn_out = pull_out(outward)
    result_rows = with_core(grad_result.astype(LOW))
    grad_active = dot_plain(result_rows, full_down_t)
    gate_low = (grad_active * gate_factor.astype(WIDE)).astype(LOW)
    upward_low = (grad_active * gelu_low.astype(WIDE)).astype(LOW)
    down_part = dot_left(result_rows, active_low).astype(LOW)
    down_sum = lax.psum_scatter(down_part, "ctx", scatter_dimension=0, tiled=True)
    hidden_part = dot_right(gate_low, full_gate) + dot_right(upward_low, full_up)
    hidden_given = hidden_part[span:].astype(LOW)
    hidden_mine = (
        hidden_part[:span] + swapped(hidden_given, "core").astype(WIDE)
    ).astype(LOW)
    hidden_theirs = swapped(hidden_mine, "tensor")

    ffn_turned = after(ffn_rows, hidden_given)
    ffn_turned = ffn_turned.reshape(2 * span, 4, 4, zrows).transpose(2, 0, 1, 3)
    ffn_turned = ffn_turned.reshape(4, 2 * span, width)
    both_low = jnp.concatenate([gate_low, upward_low], axis=1)
    pair_terms = [
        dot_left(
            lax.dynamic_index_in_dim(ffn_turned, lax.rem(z + j, 4), 0, keepdims=False), both_low
        ).astype(LOW)
        for j in (2, 1, 3, 0)
    ]
    pair_sum = ring_scatter([pair_terms[3], pair_terms[1], pair_terms[0], pair_terms[2]], "z")

    grad_ffn_in = hidden_mine.astype(WIDE) + hidden_theirs.astype(WIDE)
    unused, pull_ffn_norm = jax.vjp(rms_norm, hidden, norm_ffn_in)
    grad_hidden_norm, grad_gain_ffn_in = pull_ffn_norm(grad_ffn_in)
    grad_hidden = outward + grad_hidden_norm

    unused, pull_attn_norm = jax.vjp(rms_norm, branch, norm_attn)
    grad_branch, grad_gain_attn_out = pull_attn_norm(grad_hidden)
    branch_low = grad_branch.astype(LOW)
    grad_attended = dot_plain(branch_low, full_out_t).reshape(span, heads, head_size).astype(LOW)
    grad_probs = jnp.einsum(
        "chd,kd->hck", grad_attended, all_values, preferred_element_type=WIDE
    )
    grad_scores = (
        probs * (grad_probs - jnp.sum(probs * grad_probs, axis=-1, keepdims=True))
    ).astype(LOW)
    grad_queries = jnp.einsum("hck,kd->chd", grad_scores, all_keys, preferred_element_type=WIDE)
    grad_keys = jnp.einsum("hck,chd->kd", grad_scores, query_low, preferred_element_type=WIDE)
    grad_values = jnp.einsum(
        "hck,chd->kd", probs_low, grad_attended, preferred_element_type=WIDE
    )
    grad_kv = jnp.concatenate([grad_keys, grad_values], axis=1)
    grad_kv_low = grad_kv[:reach].astype(LOW)
    own_kv = (
        grad_kv[reach:]
        + send(grad_kv_low[span:], "ctx", [(1, 0), (2, 1), (3, 2)]).astype(WIDE)
        + send(grad_kv_low[:span], "ctx", [(2, 0), (3, 1)]).astype(WIDE)
    )
    unused, pull_query = jax.vjp(query_prep, query_raw, norm_query)
    grad_query_raw, grad_gain_query = pull_query(grad_queries)
    query_grad_low = grad_query_raw.reshape(span, heads * head_size).astype(LOW)
    unused, pull_key = jax.vjp(key_prep, key_raw, norm_key)
    grad_key_raw, grad_gain_key = pull_key(own_kv[:, :head_size])
    kv_grad_low = jnp.concatenate([grad_key_raw, own_kv[:, head_size:]], axis=1).astype(LOW)
    normed_part = dot_right(query_grad_low, full_query) + dot_right(kv_grad_low, full_kv)
    unused, pull_gain = jax.vjp(lambda gain: rms_norm(inputs, gain), norm_in)
    (grad_gain_in,) = pull_gain(normed_part)
    normed_mine = normed_part.astype(LOW)
    normed_theirs = swapped(normed_mine, "tensor")

    own_terms = jnp.concatenate(
        [
            dot_left(normed_low, query_grad_low).astype(LOW).reshape(4, width, -1),
            dot_left(branch_low, attended_low).astype(LOW).reshape(4, width, -1),
        ],
        axis=1,
    )
    def gain_grad_rows(grad, blocks):
        grad = grad.reshape(4, 1, blocks)
        return jnp.pad(grad, ((0, 0), (0, 0), (0, 512 - blocks)))

    gain_terms = jnp.concatenate(
        [
            gain_grad_rows(grad_gain_in, width),
            gain_grad_rows(0.5 * grad_gain_attn_out, width),
            gain_grad_rows(0.5 * grad_gain_ffn_in, width),
            gain_grad_rows(0.5 * grad_gain_ffn_out, width),
            gain_grad_rows(grad_gain_query, head_size // 4),
            gain_grad_rows(grad_gain_key, head_size // 4),
            jnp.zeros((4, 26, 512), WIDE),
        ],
        axis=1,
    ).astype(LOW)
    shared_terms = jnp.concatenate(
        [
            dot_left(normed_low, kv_grad_low).astype(LOW).reshape(4, width, -1),
            gain_terms,
        ],
        axis=1,
    )
    terms = jnp.concatenate(
        [own_terms.reshape(4, 2, 4, -1, 512), shared_terms.reshape(4, 2, 4, -1, 512)], axis=3
    )
    split = own_terms.shape[1] // 8
    kept = jnp.where(first_core, terms[:, 0], terms[:, 1])
    given = jnp.where(first_core, terms[:, 1], terms[:, 0])
    attn_sum = exchanged_sum(add(kept, swapped(given, "core")), "ctx")

    output = hidden + rms_norm(result, norm_ffn_out)
    grad_normed = normed_mine.astype(WIDE) + normed_theirs.astype(WIDE)
    unused, pull_in = jax.vjp(lambda v: rms_norm(v, norm_in), inputs)
    (grad_inputs_norm,) = pull_in(grad_normed)
    grad_inputs = grad_hidden + grad_inputs_norm

    def both_cores(x, other):
        return jnp.concatenate(
            [jnp.where(first_core, x, other), jnp.where(first_core, other, x)], axis=-1
        ).astype(WIDE)

    down_sum = exchanged_sum(down_sum.reshape(4, zrows, hidden_half), "z")
    down_sum = add(down_sum, swapped(down_sum, "xl"))
    down_sum = lax.all_gather(down_sum, "z", axis=0, tiled=True)
    grad_w_down = both_cores(down_sum, swapped(down_sum, "core")).T

    pair_sum = exchanged_sum(pair_sum.reshape(4, zrows, 2 * hidden_half), "ctx")
    pair_sum = add(pair_sum, swapped(pair_sum, "xl"))
    pair_previous = send(pair_sum, "z", RING)
    pair_following = send(pair_sum, "z", BACK)
    h = middle(zrows)
    pair_opposite = jnp.concatenate(
        [send(pair_previous[:h], "z", RING), send(pair_following[h:], "z", BACK)], axis=0
    )
    pair_sum = absolute([pair_sum, pair_following, pair_opposite, pair_previous], z, 0)
    pair_sum = pair_sum.reshape(width, 2 * hidden_half)
    pair_other = swapped(pair_sum, "core")
    grad_w_gate = both_cores(pair_sum[:, :hidden_half], pair_other[:, :hidden_half])
    grad_w_up = both_cores(pair_sum[:, hidden_half:], pair_other[:, hidden_half:])

    attn_sum = exchanged_sum(attn_sum, "z")
    attn_sum = add(attn_sum, swapped(attn_sum, "xl"))
    shared = attn_sum[split:]
    attn_sum = jnp.concatenate([attn_sum[:split], add(shared, swapped(shared, "tensor"))], axis=0)
    attn_sum = absolute(direct_gather(attn_sum, "z"), z, 0)
    other_sum = swapped(attn_sum, "core")
    attn_sum = jnp.stack(
        [
            jnp.where(first_core, attn_sum, other_sum),
            jnp.where(first_core, other_sum, attn_sum),
        ]
    ).astype(WIDE)
    own_sums = attn_sum[:, :, :split].reshape(2 * width, 512)
    shared_sums = attn_sum[:, :, split:].reshape(width + 32, 512)
    gain_sums = shared_sums[width:]

    return (
        output.astype(LOW)[None],
        grad_inputs[None],
        own_sums[:width],
        shared_sums[:width, :head_size],
        shared_sums[:width, head_size:],
        own_sums[width:].T,
        grad_w_gate,
        grad_w_up,
        grad_w_down,
        gain_sums[0, :width],
        gain_sums[1, :width],
        gain_sums[4, : head_size // 4],
        gain_sums[5, : head_size // 4],
        gain_sums[2, :width],
        gain_sums[3, :width],
    )


def solution(mesh):
    parts = Mesh(mesh.devices.reshape(4, 2, 2, 4, 2), ("z", "xl", "core", "ctx", "tensor"))
    rep = ("z", "xl", "core")
    return jax.shard_map(
        shards,
        mesh=parts,
        in_specs=(
            P(rep, "ctx", None),
            P(rep, None),
            P("ctx", "tensor"),
            P("ctx", None),
            P("ctx", None),
            P("tensor", "ctx"),
            P("ctx", "tensor"),
            P("ctx", "tensor"),
            P("tensor", "ctx"),
            P("ctx"),
            P("ctx"),
            P("ctx"),
            P("ctx"),
            P("ctx"),
            P("ctx"),
            P(rep, "ctx", None),
        ),
        out_specs=(
            P(rep, "ctx", None),
            P(rep, "ctx", None),
            P("ctx", "tensor"),
            P("ctx", None),
            P("ctx", None),
            P("tensor", "ctx"),
            P("ctx", "tensor"),
            P("ctx", "tensor"),
            P("tensor", "ctx"),
            P("ctx"),
            P("ctx"),
            P("ctx"),
            P("ctx"),
            P("ctx"),
            P("ctx"),
        ),
        check_vma=False,
    )
```

```python
import jax
import jax.numpy as jnp
from jax import lax
from jax.sharding import Mesh
from jax.sharding import PartitionSpec as P

WINDOW = 512
EPSILON = 1e-06
ROTARY_BASE = 10000.0
MASKED = -1e30
GELU = 0.7978845608028654
LOW = jnp.bfloat16
WIDE = jnp.float32

RING = [(i, (i + 1) % 4) for i in range(4)]
BACK = [(i, (i - 1) % 4) for i in range(4)]
ACROSS = [(i, (i + 2) % 4) for i in range(4)]
SWAP = [(0, 1), (1, 0)]


def send(x, axis, pairs):
    return lax.ppermute(x, axis, pairs)


def swapped(x, axis):
    return lax.ppermute(x, axis, SWAP)


def after(x, *others):
    return lax.optimization_barrier((x, *others))[0]


def middle(rows):
    return rows // 2 if rows < 16 else rows // 16 * 8


def direct_gather(x, axis):
    previous = send(x, axis, RING)
    following = send(x, axis, BACK)
    opposite = send(x, axis, ACROSS)
    return [x, following, opposite, previous]


def ring_scatter(blocks, axis):
    own, following, opposite, previous = blocks
    h = middle(own.shape[0])
    above = send(opposite[:h], axis, RING)
    below = send(opposite[h:], axis, BACK)
    following = jnp.concatenate([add(following[:h], above), following[h:]], axis=0)
    previous = jnp.concatenate([previous[:h], add(previous[h:], below)], axis=0)
    from_previous = send(following, axis, RING)
    from_following = send(previous, axis, BACK)
    total = own.astype(WIDE) + from_previous.astype(WIDE) + from_following.astype(WIDE)
    return total.astype(LOW)


def exchanged_sum(x, axis):
    moved = lax.all_to_all(x, axis, split_axis=0, concat_axis=0, tiled=True)
    return moved.astype(WIDE).sum(axis=0).astype(LOW)


def add(a, b):
    return (a.astype(WIDE) + b.astype(WIDE)).astype(LOW)


def absolute(blocks, at, dim):
    whole = jnp.zeros(
        blocks[0].shape[:dim] + (4,) + blocks[0].shape[dim:], blocks[0].dtype
    )
    for j, block in enumerate(blocks):
        whole = lax.dynamic_update_index_in_dim(whole, block, lax.rem(at + j, 4), dim)
    return whole


def rms_norm(values, gain):
    scale = lax.rsqrt(jnp.mean(values * values, axis=-1, keepdims=True) + EPSILON)
    return values * scale * gain


def rotate(values, cosine, sine):
    half = values.shape[-1] // 2
    first = values[..., :half]
    second = values[..., half:]
    return jnp.concatenate(
        [first * cosine - second * sine, second * cosine + first * sine], axis=-1
    )


def dot_plain(left, right):
    return jnp.dot(left, right, preferred_element_type=WIDE)


def dot_right(left, right):
    return lax.dot_general(left, right, (((1,), (1,)), ((), ())), preferred_element_type=WIDE)


def dot_left(left, right):
    return lax.dot_general(left, right, (((0,), (0,)), ((), ())), preferred_element_type=WIDE)


def with_core(x):
    return jnp.concatenate([x, swapped(x, "core")], axis=0)


def shards(
    tokens,
    doc_ids,
    w_query,
    w_key,
    w_value,
    w_out,
    w_gate,
    w_up,
    w_down,
    gain_in,
    gain_attn_out,
    gain_query,
    gain_key,
    gain_ffn_in,
    gain_ffn_out,
    cotangent,
):
    c = lax.axis_index("ctx")
    z = lax.axis_index("z")
    first_core = lax.axis_index("core") == 0
    width = w_query.shape[0]
    model = 4 * width
    head_size = w_key.shape[1]
    heads = w_query.shape[1] // head_size
    zrows = width // 4
    span = tokens.shape[1]

    def gain_row(gain):
        return jnp.pad(gain, (0, 512 - gain.shape[-1]))[None]

    gain_rows = jnp.concatenate(
        [
            gain_row(gain)
            for gain in (gain_in, gain_attn_out, gain_ffn_in, gain_ffn_out, gain_query, gain_key)
        ]
        + [jnp.zeros((2, 512), LOW)],
        axis=0,
    )
    w_out_t = w_out.T
    w_kv = jnp.concatenate([w_key, w_value], axis=1)
    half_out = width // 2
    attn_own = jnp.concatenate(
        [
            jnp.where(first_core, w_query, w_kv),
            jnp.where(first_core, w_out_t[:half_out], w_out_t[half_out:]),
            gain_rows,
        ],
        axis=0,
    )
    attn_stack = absolute(direct_gather(attn_own, "ctx"), c, 0)
    swap_rows = width + half_out
    mine = attn_stack[:, :swap_rows]
    theirs = swapped(mine, "core")
    full_query = jnp.where(first_core, mine[:, :width], theirs[:, :width]).reshape(model, -1)
    full_kv = jnp.where(first_core, theirs[:, :width], mine[:, :width]).reshape(model, -1)
    full_out_t = jnp.concatenate(
        [
            jnp.where(first_core, mine[:, width:], theirs[:, width:]),
            jnp.where(first_core, theirs[:, width:], mine[:, width:]),
        ],
        axis=1,
    ).reshape(model, -1)
    gain_table = attn_stack[:, swap_rows:].astype(WIDE)
    norm_in, norm_attn, norm_ffn_in, norm_ffn_out = (
        gain_table[:, k, :width].reshape(model) for k in range(4)
    )
    norm_query, norm_key = (
        gain_table[:, k, : head_size // 4].reshape(head_size) for k in (4, 5)
    )

    hidden = w_gate.shape[1]
    share = (hidden // 2 + 127) // 128 * 128

    def core_half(x):
        return jnp.where(
            first_core,
            x[:, :share],
            jnp.pad(x[:, share:], ((0, 0), (0, 2 * share - hidden))),
        )

    gate_up_own = jnp.concatenate([core_half(w_gate), core_half(w_up)], axis=1)
    full_gate_up = lax.all_gather(gate_up_own, "ctx", axis=0, tiled=True)
    down_own = core_half(w_down.T)
    down_part = lax.dynamic_slice_in_dim(down_own, z * zrows, zrows, axis=0)
    down_rest = direct_gather(down_part, "ctx")[1:]

    inputs = tokens[0].astype(WIDE)
    outward = cotangent[0].astype(WIDE)
    start = c * span
    doc_row = doc_ids[0]
    reach = 2 * span
    query_docs = lax.dynamic_slice_in_dim(doc_row, start, span)
    query_at = start + jnp.arange(span, dtype=jnp.int32)
    earlier = jnp.sum((doc_row[None, :] < query_docs[:, None]).astype(jnp.int32), axis=1)
    places = (query_at - earlier).astype(WIDE)
    half = head_size // 2
    freqs = ROTARY_BASE ** (-2.0 * jnp.arange(half, dtype=WIDE) / head_size)
    angles = places[:, None] * freqs[None, :]
    cosine = jnp.cos(angles)
    sine = jnp.sin(angles)
    padded_docs = jnp.concatenate([jnp.full((reach,), -1, jnp.int32), doc_row])
    key_docs = lax.dynamic_slice_in_dim(padded_docs, start, reach + span)
    key_at = start - reach + jnp.arange(reach + span, dtype=jnp.int32)
    allowed = (
        (query_docs[:, None] == key_docs[None, :])
        & (key_at[None, :] <= query_at[:, None])
        & (query_at[:, None] - key_at[None, :] < WINDOW)
    )

    cosine_rows = jnp.concatenate([cosine] * heads, axis=0)
    sine_rows = jnp.concatenate([sine] * heads, axis=0)
    allowed_rows = jnp.concatenate([allowed] * heads, axis=0)

    def stacked(x):
        return jnp.concatenate(
            [x[:, k * head_size : (k + 1) * head_size] for k in range(heads)], axis=0
        )

    def side_by_side(x):
        return jnp.concatenate([x[k * span : (k + 1) * span] for k in range(heads)], axis=1)

    def query_prep(raw, gain):
        return rotate(rms_norm(raw, gain), cosine_rows, sine_rows) * head_size ** (-0.5)

    def key_prep(raw, gain):
        return rotate(rms_norm(raw, gain), cosine, sine)

    normed_low = rms_norm(inputs, norm_in).astype(LOW)
    kv_raw = dot_plain(normed_low, full_kv)
    key_raw = kv_raw[:, :head_size]
    key_low = key_prep(key_raw, norm_key).astype(LOW)
    value_low = kv_raw[:, head_size:].astype(LOW)
    kv_low = jnp.concatenate([key_low, value_low], axis=1)
    before2 = send(kv_low, "ctx", [(0, 2), (1, 3)])
    before1 = send(kv_low, "ctx", [(0, 1), (1, 2), (2, 3)])
    query_raw = stacked(dot_plain(normed_low, full_query))
    query_low = query_prep(query_raw, norm_query).astype(LOW)
    down_rest = jnp.stack(lax.optimization_barrier((*down_rest, query_low))[:3])
    down_previous = send(down_rest, "z", RING)
    down_following = send(down_rest, "z", BACK)
    all_kv = jnp.concatenate([before2, before1, kv_low], axis=0)
    all_keys = all_kv[:, :head_size]
    all_values = all_kv[:, head_size:]
    scores = jnp.where(allowed_rows, dot_right(query_low, all_keys), MASKED)
    largest = jnp.max(scores, axis=-1, keepdims=True)
    total_log = largest + jnp.log(jnp.sum(jnp.exp(scores - largest), axis=-1, keepdims=True))
    probs = jnp.exp(scores - total_log)
    probs_low = probs.astype(LOW)
    attended_low = side_by_side(dot_plain(probs_low, all_values)).astype(LOW)
    branch_mine = dot_right(attended_low, full_out_t).astype(LOW)
    branch_theirs = swapped(branch_mine, "tensor")
    down_previous, down_following = lax.optimization_barrier(
        (down_previous, down_following, branch_mine)
    )[:2]
    h = middle(zrows)
    down_opposite = jnp.concatenate(
        [
            send(down_previous[:, :h], "z", RING),
            send(down_following[:, h:], "z", BACK),
        ],
        axis=1,
    )
    branch = branch_mine.astype(WIDE) + branch_theirs.astype(WIDE)
    between = inputs + rms_norm(branch, norm_attn)

    ffn_in_low = rms_norm(between, norm_ffn_in).astype(LOW)
    ffn_rows = with_core(ffn_in_low)
    gate_up = dot_plain(ffn_rows, full_gate_up)
    gate = gate_up[:, :share]
    upward = gate_up[:, share:]
    bend = GELU * (1.0 + 0.134145 * gate * gate)
    level = jnp.tanh(GELU * gate * (1.0 + 0.044715 * gate * gate))
    gelu = 0.5 * gate * (1.0 + level)
    gelu_slope = 0.5 * (1.0 + level) + 0.5 * gate * (1.0 - level * level) * bend
    active_low, gelu_low, gate_factor = lax.optimization_barrier(
        (
            (gelu * upward).astype(LOW),
            gelu.astype(LOW),
            (upward * gelu_slope).astype(LOW),
        )
    )
    down_rest = absolute([down_rest, down_following, down_opposite, down_previous], z, 1)
    down_rest = down_rest.reshape(3, width, share)
    full_down_t = absolute([down_own] + [down_rest[j] for j in range(3)], c, 0)
    full_down_t = full_down_t.reshape(model, share)
    result_part = dot_right(active_low, full_down_t)
    result_given = result_part[span:].astype(LOW)
    result_mine = (
        result_part[:span] + swapped(result_given, "core").astype(WIDE)
    ).astype(LOW)
    result = result_mine.astype(WIDE) + swapped(result_mine, "tensor").astype(WIDE)
    unused, pull_out = jax.vjp(rms_norm, result, norm_ffn_out)
    grad_result, grad_gain_ffn_out = pull_out(outward)
    result_rows = with_core(grad_result.astype(LOW))
    grad_active = dot_plain(result_rows, full_down_t)
    gate_low, upward_low = lax.optimization_barrier(
        (
            (grad_active * gate_factor.astype(WIDE)).astype(LOW),
            (grad_active * gelu_low.astype(WIDE)).astype(LOW),
        )
    )
    down_grad = dot_left(result_rows, active_low).astype(LOW)
    down_sum = lax.psum_scatter(down_grad, "ctx", scatter_dimension=0, tiled=True)
    both_low = after(jnp.concatenate([gate_low, upward_low], axis=1), down_grad)
    hidden_part = dot_right(both_low, full_gate_up)
    hidden_given = hidden_part[span:].astype(LOW)
    hidden_mine = (
        hidden_part[:span] + swapped(hidden_given, "core").astype(WIDE)
    ).astype(LOW)

    ffn_wait = after(ffn_rows, hidden_given)
    gate_grad = dot_left(ffn_wait, gate_low).astype(LOW)
    gate_sum = lax.psum_scatter(gate_grad, "ctx", scatter_dimension=0, tiled=True)
    ffn_turned = ffn_wait.reshape(2 * span, 4, 4, zrows).transpose(2, 0, 1, 3)
    ffn_turned = ffn_turned.reshape(4, 2 * span, width)
    up_terms = [
        dot_left(
            lax.dynamic_index_in_dim(ffn_turned, lax.rem(z + j, 4), 0, keepdims=False),
            upward_low,
        ).astype(LOW)
        for j in range(4)
    ]
    up_sum = ring_scatter(up_terms, "z")

    hidden_theirs = swapped(hidden_mine, "tensor")
    grad_ffn_in = hidden_mine.astype(WIDE) + hidden_theirs.astype(WIDE)
    unused, pull_ffn_norm = jax.vjp(rms_norm, between, norm_ffn_in)
    grad_hidden_norm, grad_gain_ffn_in = pull_ffn_norm(grad_ffn_in)
    grad_hidden = outward + grad_hidden_norm

    unused, pull_attn_norm = jax.vjp(rms_norm, branch, norm_attn)
    grad_branch, grad_gain_attn_out = pull_attn_norm(grad_hidden)
    branch_low = grad_branch.astype(LOW)
    grad_attended = stacked(dot_plain(branch_low, full_out_t).astype(LOW))
    grad_probs = dot_right(grad_attended, all_values)
    grad_scores = (
        probs * (grad_probs - jnp.sum(probs * grad_probs, axis=-1, keepdims=True))
    ).astype(LOW)
    grad_keys = dot_left(grad_scores, query_low)
    grad_values = dot_left(probs_low, grad_attended)
    grad_kv = jnp.concatenate([grad_keys, grad_values], axis=1)
    grad_kv_low = grad_kv[:reach].astype(LOW)
    back1 = send(grad_kv_low[span:], "ctx", [(1, 0), (2, 1), (3, 2)])
    back2 = send(grad_kv_low[:span], "ctx", [(2, 0), (3, 1)])
    grad_queries = dot_plain(grad_scores, all_keys)
    unused, pull_query = jax.vjp(query_prep, query_raw, norm_query)
    grad_query_raw, grad_gain_query = pull_query(grad_queries)
    query_grad_low = side_by_side(grad_query_raw).astype(LOW)
    own_kv = grad_kv[reach:] + back1.astype(WIDE) + back2.astype(WIDE)
    unused, pull_key = jax.vjp(key_prep, key_raw, norm_key)
    grad_key_raw, grad_gain_key = pull_key(own_kv[:, :head_size])
    kv_grad_low = jnp.concatenate([grad_key_raw, own_kv[:, head_size:]], axis=1).astype(LOW)
    normed_part = dot_right(query_grad_low, full_query) + dot_right(kv_grad_low, full_kv)
    unused, pull_gain = jax.vjp(lambda gain: rms_norm(inputs, gain), norm_in)
    (grad_gain_in,) = pull_gain(normed_part)
    normed_mine = normed_part.astype(LOW)
    normed_theirs = swapped(normed_mine, "tensor")

    own_terms = jnp.concatenate(
        [
            dot_left(normed_low, query_grad_low).astype(LOW).reshape(4, width, -1),
            dot_left(branch_low, attended_low).astype(LOW).reshape(4, width, -1),
        ],
        axis=1,
    )
    head_gain_grads = jnp.concatenate(
        [grad_gain_query.reshape(4, -1), grad_gain_key.reshape(4, -1)], axis=1
    )
    head_gain_grads = jnp.pad(
        head_gain_grads, ((0, 0), (0, width - head_gain_grads.shape[1]))
    ).reshape(model)
    gain_grads = jnp.stack(
        [
            grad_gain_in,
            0.5 * grad_gain_attn_out,
            0.5 * grad_gain_ffn_in,
            0.5 * grad_gain_ffn_out,
            head_gain_grads,
            jnp.zeros_like(grad_gain_in),
            jnp.zeros_like(grad_gain_in),
            jnp.zeros_like(grad_gain_in),
        ]
    )
    gain_terms = jnp.stack(
        [
            jnp.pad(gain_grads[:, k * width : (k + 1) * width], ((0, 24), (0, 512 - width)))
            for k in range(4)
        ]
    ).astype(LOW)
    shared_terms = jnp.concatenate(
        [
            dot_left(normed_low, kv_grad_low).astype(LOW).reshape(4, width, -1),
            gain_terms,
        ],
        axis=1,
    )
    terms = jnp.concatenate(
        [own_terms.reshape(4, 2, 4, -1, 512), shared_terms.reshape(4, 2, 4, -1, 512)], axis=3
    )
    split = own_terms.shape[1] // 8
    kept = jnp.where(first_core, terms[:, 0], terms[:, 1])
    given = jnp.where(first_core, terms[:, 1], terms[:, 0])
    attn_sum = exchanged_sum(add(kept, swapped(given, "core")), "ctx")

    output = between + rms_norm(result, norm_ffn_out)
    grad_normed = normed_mine.astype(WIDE) + normed_theirs.astype(WIDE)
    unused, pull_in = jax.vjp(lambda v: rms_norm(v, norm_in), inputs)
    (grad_inputs_norm,) = pull_in(grad_normed)
    grad_inputs = grad_hidden + grad_inputs_norm

    def both_cores(x, other):
        return jnp.concatenate(
            [
                jnp.where(first_core, x, other),
                jnp.where(first_core, other, x)[:, : hidden - share],
            ],
            axis=-1,
        ).astype(WIDE)

    down_sum = exchanged_sum(down_sum.reshape(4, zrows, share), "z")
    down_sum = add(down_sum, swapped(down_sum, "xl"))
    down_sum = absolute(direct_gather(down_sum, "z"), z, 0).reshape(width, share)
    grad_w_down = both_cores(down_sum, swapped(down_sum, "core")).T

    up_sum = exchanged_sum(up_sum.reshape(4, zrows, share), "ctx")
    gate_sum = exchanged_sum(gate_sum.reshape(4, zrows, share), "z")
    pair_sum = jnp.concatenate([gate_sum, up_sum], axis=1)
    pair_sum = add(pair_sum, swapped(pair_sum, "xl"))
    pair_sum = absolute(direct_gather(pair_sum, "z"), z, 0).reshape(width, 2 * share)
    pair_other = swapped(pair_sum, "core")
    grad_w_gate = both_cores(pair_sum[:, :share], pair_other[:, :share])
    grad_w_up = both_cores(pair_sum[:, share:], pair_other[:, share:])

    attn_sum = exchanged_sum(attn_sum, "z")
    attn_sum = add(attn_sum, swapped(attn_sum, "xl"))
    shared = attn_sum[split:]
    attn_sum = jnp.concatenate([attn_sum[:split], add(shared, swapped(shared, "tensor"))], axis=0)
    attn_sum = absolute(direct_gather(attn_sum, "z"), z, 0)
    other_sum = swapped(attn_sum, "core")
    attn_sum = jnp.stack(
        [
            jnp.where(first_core, attn_sum, other_sum),
            jnp.where(first_core, other_sum, attn_sum),
        ]
    ).astype(WIDE)
    own_sums = attn_sum[:, :, :split].reshape(2 * width, 512)
    shared_sums = attn_sum[:, :, split:].reshape(width + 32, 512)
    gain_sums = shared_sums[width:]

    return (
        output.astype(LOW)[None],
        grad_inputs[None],
        own_sums[:width],
        shared_sums[:width, :head_size],
        shared_sums[:width, head_size:],
        own_sums[width:].T,
        grad_w_gate,
        grad_w_up,
        grad_w_down,
        gain_sums[0, :width],
        gain_sums[1, :width],
        gain_sums[4, : head_size // 4],
        gain_sums[4, head_size // 4 : head_size // 2],
        gain_sums[2, :width],
        gain_sums[3, :width],
    )


def solution(mesh):
    parts = Mesh(mesh.devices.reshape(4, 2, 2, 4, 2), ("z", "xl", "core", "ctx", "tensor"))
    rep = ("z", "xl", "core")
    return jax.shard_map(
        shards,
        mesh=parts,
        in_specs=(
            P(rep, "ctx", None),
            P(rep, None),
            P("ctx", "tensor"),
            P("ctx", None),
            P("ctx", None),
            P("tensor", "ctx"),
            P("ctx", "tensor"),
            P("ctx", "tensor"),
            P("tensor", "ctx"),
            P("ctx"),
            P("ctx"),
            P("ctx"),
            P("ctx"),
            P("ctx"),
            P("ctx"),
            P(rep, "ctx", None),
        ),
        out_specs=(
            P(rep, "ctx", None),
            P(rep, "ctx", None),
            P("ctx", "tensor"),
            P("ctx", None),
            P("ctx", None),
            P("tensor", "ctx"),
            P("ctx", "tensor"),
            P("ctx", "tensor"),
            P("tensor", "ctx"),
            P("ctx"),
            P("ctx"),
            P("ctx"),
            P("ctx"),
            P("ctx"),
            P("ctx"),
        ),
        check_vma=False,
    )
```

```python
import jax
import jax.numpy as jnp
from jax import lax
from jax.sharding import Mesh
from jax.sharding import PartitionSpec as P

WINDOW = 512
EPSILON = 1e-06
ROTARY_BASE = 10000.0
MASKED = -1e30
GELU = 0.7978845608028654
LOW = jnp.bfloat16
WIDE = jnp.float32

RING = [(i, (i + 1) % 4) for i in range(4)]
BACK = [(i, (i - 1) % 4) for i in range(4)]
ACROSS = [(i, (i + 2) % 4) for i in range(4)]
SWAP = [(0, 1), (1, 0)]


def send(x, axis, pairs):
    return lax.ppermute(x, axis, pairs)


def swapped(x, axis):
    return lax.ppermute(x, axis, SWAP)


def after(x, *others):
    return lax.optimization_barrier((x, *others))[0]


def direct_gather(x, axis):
    previous = send(x, axis, RING)
    following = send(x, axis, BACK)
    opposite = send(x, axis, ACROSS)
    return [x, following, opposite, previous]


def exchanged_sum(x, axis):
    moved = lax.all_to_all(x, axis, split_axis=0, concat_axis=0, tiled=True)
    return moved.astype(WIDE).sum(axis=0).astype(LOW)


def add(a, b):
    return (a.astype(WIDE) + b.astype(WIDE)).astype(LOW)


def absolute(blocks, at, dim):
    whole = jnp.zeros(
        blocks[0].shape[:dim] + (4,) + blocks[0].shape[dim:], blocks[0].dtype
    )
    for j, block in enumerate(blocks):
        whole = lax.dynamic_update_index_in_dim(whole, block, lax.rem(at + j, 4), dim)
    return whole


def rms_norm(values, gain):
    scale = lax.rsqrt(jnp.mean(values * values, axis=-1, keepdims=True) + EPSILON)
    return values * scale * gain


def rotate(values, cosine, sine):
    half = values.shape[-1] // 2
    first = values[..., :half]
    second = values[..., half:]
    return jnp.concatenate(
        [first * cosine - second * sine, second * cosine + first * sine], axis=-1
    )


def dot_plain(left, right):
    return jnp.dot(left, right, preferred_element_type=WIDE)


def dot_right(left, right):
    return lax.dot_general(left, right, (((1,), (1,)), ((), ())), preferred_element_type=WIDE)


def dot_left(left, right):
    return lax.dot_general(left, right, (((0,), (0,)), ((), ())), preferred_element_type=WIDE)


def with_core(x):
    return jnp.concatenate([x, swapped(x, "core")], axis=0)


def shards(
    tokens,
    doc_ids,
    w_query,
    w_key,
    w_value,
    w_out,
    w_gate,
    w_up,
    w_down,
    gain_in,
    gain_attn_out,
    gain_query,
    gain_key,
    gain_ffn_in,
    gain_ffn_out,
    cotangent,
):
    c = lax.axis_index("ctx")
    z = lax.axis_index("z")
    first_core = lax.axis_index("core") == 0
    width = w_query.shape[0]
    model = 4 * width
    head_size = w_key.shape[1]
    heads = w_query.shape[1] // head_size
    zrows = width // 4
    span = tokens.shape[1]

    hidden = w_gate.shape[1]
    share = (hidden // 2 + 127) // 128 * 128
    half_out = width // 2
    w_out_t = w_out.T
    w_kv = jnp.concatenate([w_key, w_value], axis=1)
    query_or_kv_own = jnp.where(first_core, w_query, w_kv)
    query_or_kv = direct_gather(query_or_kv_own, "ctx")

    def core_share(x):
        x = lax.dynamic_slice_in_dim(x, z * zrows, zrows, axis=0)
        return jnp.where(
            first_core,
            x[:, :share],
            jnp.pad(x[:, share:], ((0, 0), (0, 2 * share - hidden))),
        )

    ffn_own = jnp.concatenate(
        [core_share(w_gate), core_share(w_up), core_share(w_down.T)], axis=1
    )
    full_ffn = lax.all_gather(ffn_own, ("ctx", "z"), axis=0, tiled=True)
    full_gate_up = full_ffn[:, : 2 * share]
    full_down_t = full_ffn[:, 2 * share :]

    def gain_row(gain):
        return jnp.pad(gain, (0, 512 - gain.shape[-1]))[None]

    gain_rows = jnp.concatenate(
        [
            gain_row(gain)
            for gain in (gain_in, gain_attn_out, gain_ffn_in, gain_ffn_out, gain_query, gain_key)
        ]
        + [jnp.zeros((2, 512), LOW)],
        axis=0,
    )
    gain_rows = after(gain_rows, query_or_kv_own)
    out_half = jnp.where(first_core, w_out_t[:half_out], w_out_t[half_out:])
    out_half = after(out_half, gain_rows)
    gain_table = absolute(direct_gather(gain_rows, "ctx"), c, 0).astype(WIDE)
    out_halves = direct_gather(out_half, "ctx")
    mine = absolute(query_or_kv, c, 0)
    theirs = swapped(mine, "core")
    full_query = jnp.where(first_core, mine, theirs).reshape(model, -1)
    full_kv = jnp.where(first_core, theirs, mine).reshape(model, -1)
    out_mine = absolute(out_halves, c, 0)
    out_theirs = swapped(out_mine, "core")
    full_out_t = jnp.concatenate(
        [
            jnp.where(first_core, out_mine, out_theirs),
            jnp.where(first_core, out_theirs, out_mine),
        ],
        axis=1,
    ).reshape(model, -1)
    norm_in, norm_attn, norm_ffn_in, norm_ffn_out = (
        gain_table[:, k, :width].reshape(model) for k in range(4)
    )
    norm_query, norm_key = (
        gain_table[:, k, : head_size // 4].reshape(head_size) for k in (4, 5)
    )

    inputs = tokens[0].astype(WIDE)
    outward = cotangent[0].astype(WIDE)
    start = c * span
    doc_row = doc_ids[0]
    reach = 2 * span
    query_docs = lax.dynamic_slice_in_dim(doc_row, start, span)
    query_at = start + jnp.arange(span, dtype=jnp.int32)
    earlier = jnp.sum((doc_row[None, :] < query_docs[:, None]).astype(jnp.int32), axis=1)
    places = (query_at - earlier).astype(WIDE)
    half = head_size // 2
    freqs = ROTARY_BASE ** (-2.0 * jnp.arange(half, dtype=WIDE) / head_size)
    angles = places[:, None] * freqs[None, :]
    cosine = jnp.cos(angles)
    sine = jnp.sin(angles)
    padded_docs = jnp.concatenate([jnp.full((reach,), -1, jnp.int32), doc_row])
    key_docs = lax.dynamic_slice_in_dim(padded_docs, start, reach + span)
    key_at = start - reach + jnp.arange(reach + span, dtype=jnp.int32)
    allowed = (
        (query_docs[:, None] == key_docs[None, :])
        & (key_at[None, :] <= query_at[:, None])
        & (query_at[:, None] - key_at[None, :] < WINDOW)
    )

    cosine_rows = jnp.concatenate([cosine] * heads, axis=0)
    sine_rows = jnp.concatenate([sine] * heads, axis=0)
    allowed_rows = jnp.concatenate([allowed] * heads, axis=0)

    def stacked(x):
        return jnp.concatenate(
            [x[:, k * head_size : (k + 1) * head_size] for k in range(heads)], axis=0
        )

    def side_by_side(x):
        return jnp.concatenate([x[k * span : (k + 1) * span] for k in range(heads)], axis=1)

    def query_prep(raw, gain):
        return rotate(rms_norm(raw, gain), cosine_rows, sine_rows) * head_size ** (-0.5)

    def key_prep(raw, gain):
        return rotate(rms_norm(raw, gain), cosine, sine)

    normed_low = rms_norm(inputs, norm_in).astype(LOW)
    kv_raw = dot_plain(normed_low, full_kv)
    key_raw = kv_raw[:, :head_size]
    key_low = key_prep(key_raw, norm_key).astype(LOW)
    value_low = kv_raw[:, head_size:].astype(LOW)
    kv_low = jnp.concatenate([key_low, value_low], axis=1)
    before2 = send(kv_low, "ctx", [(0, 2), (1, 3)])
    before1 = send(kv_low, "ctx", [(0, 1), (1, 2), (2, 3)])
    query_raw = stacked(dot_plain(normed_low, full_query))
    query_low = query_prep(query_raw, norm_query).astype(LOW)
    all_kv = jnp.concatenate([before2, before1, kv_low], axis=0)
    all_keys = all_kv[:, :head_size]
    all_values = all_kv[:, head_size:]
    scores = jnp.where(allowed_rows, dot_right(query_low, all_keys), MASKED)
    largest = jnp.max(scores, axis=-1, keepdims=True)
    total_log = largest + jnp.log(jnp.sum(jnp.exp(scores - largest), axis=-1, keepdims=True))
    probs = jnp.exp(scores - total_log)
    probs_low = probs.astype(LOW)
    attended_low = side_by_side(dot_plain(probs_low, all_values)).astype(LOW)
    branch_mine = dot_right(attended_low, full_out_t).astype(LOW)
    branch_theirs = swapped(branch_mine, "tensor")
    branch = branch_mine.astype(WIDE) + branch_theirs.astype(WIDE)
    between = inputs + rms_norm(branch, norm_attn)

    ffn_in_low = rms_norm(between, norm_ffn_in).astype(LOW)
    ffn_rows = with_core(ffn_in_low)
    gate_up = dot_plain(ffn_rows, full_gate_up)
    gate = gate_up[:, :share]
    upward = gate_up[:, share:]
    bend = GELU * (1.0 + 0.134145 * gate * gate)
    level = jnp.tanh(GELU * gate * (1.0 + 0.044715 * gate * gate))
    gelu = 0.5 * gate * (1.0 + level)
    gelu_slope = 0.5 * (1.0 + level) + 0.5 * gate * (1.0 - level * level) * bend
    active_low, gelu_low, gate_factor = lax.optimization_barrier(
        (
            (gelu * upward).astype(LOW),
            gelu.astype(LOW),
            (upward * gelu_slope).astype(LOW),
        )
    )
    result_part = dot_right(active_low, full_down_t)
    result_given = result_part[span:].astype(LOW)
    result_mine = (
        result_part[:span] + swapped(result_given, "core").astype(WIDE)
    ).astype(LOW)
    result = result_mine.astype(WIDE) + swapped(result_mine, "tensor").astype(WIDE)
    unused, pull_out = jax.vjp(rms_norm, result, norm_ffn_out)
    grad_result, grad_gain_ffn_out = pull_out(outward)
    result_rows = with_core(grad_result.astype(LOW))
    grad_active = dot_plain(result_rows, full_down_t)
    gate_low, upward_low = lax.optimization_barrier(
        (
            (grad_active * gate_factor.astype(WIDE)).astype(LOW),
            (grad_active * gelu_low.astype(WIDE)).astype(LOW),
        )
    )
    both_low = jnp.concatenate([gate_low, upward_low], axis=1)
    ffn_grads = jnp.concatenate(
        [
            dot_left(ffn_rows, both_low).astype(LOW),
            dot_left(result_rows, active_low).astype(LOW),
        ],
        axis=1,
    )
    ffn_sum = lax.psum_scatter(ffn_grads, ("ctx", "z"), scatter_dimension=0, tiled=True)
    hidden_part = dot_right(after(both_low, ffn_grads), full_gate_up)
    hidden_given = hidden_part[span:].astype(LOW)
    hidden_mine = (
        hidden_part[:span] + swapped(hidden_given, "core").astype(WIDE)
    ).astype(LOW)
    hidden_theirs = swapped(hidden_mine, "tensor")
    grad_ffn_in = hidden_mine.astype(WIDE) + hidden_theirs.astype(WIDE)
    unused, pull_ffn_norm = jax.vjp(rms_norm, between, norm_ffn_in)
    grad_hidden_norm, grad_gain_ffn_in = pull_ffn_norm(grad_ffn_in)
    grad_hidden = outward + grad_hidden_norm

    unused, pull_attn_norm = jax.vjp(rms_norm, branch, norm_attn)
    grad_branch, grad_gain_attn_out = pull_attn_norm(grad_hidden)
    branch_low = grad_branch.astype(LOW)
    grad_attended = stacked(dot_plain(branch_low, full_out_t).astype(LOW))
    grad_probs = dot_right(grad_attended, all_values)
    grad_scores = (
        probs * (grad_probs - jnp.sum(probs * grad_probs, axis=-1, keepdims=True))
    ).astype(LOW)
    grad_keys = dot_left(grad_scores, query_low)
    grad_values = dot_left(probs_low, grad_attended)
    grad_kv = jnp.concatenate([grad_keys, grad_values], axis=1)
    grad_kv_low = grad_kv[:reach].astype(LOW)
    back1 = send(grad_kv_low[span:], "ctx", [(1, 0), (2, 1), (3, 2)])
    back2 = send(grad_kv_low[:span], "ctx", [(2, 0), (3, 1)])
    grad_queries = dot_plain(grad_scores, all_keys)
    unused, pull_query = jax.vjp(query_prep, query_raw, norm_query)
    grad_query_raw, grad_gain_query = pull_query(grad_queries)
    query_grad_low = side_by_side(grad_query_raw).astype(LOW)
    own_kv = grad_kv[reach:] + back1.astype(WIDE) + back2.astype(WIDE)
    unused, pull_key = jax.vjp(key_prep, key_raw, norm_key)
    grad_key_raw, grad_gain_key = pull_key(own_kv[:, :head_size])
    kv_grad_low = jnp.concatenate([grad_key_raw, own_kv[:, head_size:]], axis=1).astype(LOW)
    normed_part = dot_right(query_grad_low, full_query) + dot_right(kv_grad_low, full_kv)
    unused, pull_gain = jax.vjp(lambda gain: rms_norm(inputs, gain), norm_in)
    (grad_gain_in,) = pull_gain(normed_part)
    normed_mine = normed_part.astype(LOW)
    normed_theirs = swapped(normed_mine, "tensor")

    own_terms = jnp.concatenate(
        [
            dot_left(normed_low, query_grad_low).astype(LOW).reshape(4, width, -1),
            dot_left(branch_low, attended_low).astype(LOW).reshape(4, width, -1),
        ],
        axis=1,
    )
    head_gain_grads = jnp.concatenate(
        [grad_gain_query.reshape(4, -1), grad_gain_key.reshape(4, -1)], axis=1
    )
    head_gain_grads = jnp.pad(
        head_gain_grads, ((0, 0), (0, width - head_gain_grads.shape[1]))
    ).reshape(model)
    gain_grads = jnp.stack(
        [
            grad_gain_in,
            0.5 * grad_gain_attn_out,
            0.5 * grad_gain_ffn_in,
            0.5 * grad_gain_ffn_out,
            head_gain_grads,
            jnp.zeros_like(grad_gain_in),
            jnp.zeros_like(grad_gain_in),
            jnp.zeros_like(grad_gain_in),
        ]
    )
    gain_terms = jnp.stack(
        [
            jnp.pad(gain_grads[:, k * width : (k + 1) * width], ((0, 24), (0, 512 - width)))
            for k in range(4)
        ]
    ).astype(LOW)
    shared_terms = jnp.concatenate(
        [
            dot_left(normed_low, kv_grad_low).astype(LOW).reshape(4, width, -1),
            gain_terms,
        ],
        axis=1,
    )
    terms = jnp.concatenate(
        [own_terms.reshape(4, 2, 4, -1, 512), shared_terms.reshape(4, 2, 4, -1, 512)], axis=3
    )
    split = own_terms.shape[1] // 8
    kept = jnp.where(first_core, terms[:, 0], terms[:, 1])
    given = jnp.where(first_core, terms[:, 1], terms[:, 0])
    attn_sum = add(kept, swapped(given, "core")).reshape(16, -1, 512)
    attn_sum = exchanged_sum(attn_sum, ("ctx", "z"))

    output = between + rms_norm(result, norm_ffn_out)
    grad_normed = normed_mine.astype(WIDE) + normed_theirs.astype(WIDE)
    unused, pull_in = jax.vjp(lambda v: rms_norm(v, norm_in), inputs)
    (grad_inputs_norm,) = pull_in(grad_normed)
    grad_inputs = grad_hidden + grad_inputs_norm

    quarter = share // 2
    first_x = lax.axis_index("xl") == 0

    def columns(x, side):
        return jnp.concatenate(
            [x[:, (2 * k + side) * quarter : (2 * k + side + 1) * quarter] for k in range(3)],
            axis=1,
        )

    ffn_sum = after(ffn_sum, attn_sum)
    low_side = columns(ffn_sum, 0)
    high_side = columns(ffn_sum, 1)
    ffn_sum = add(
        jnp.where(first_x, low_side, high_side),
        swapped(jnp.where(first_x, high_side, low_side), "xl"),
    )
    ffn_all = lax.all_gather(ffn_sum, ("core", "xl", "z"), axis=0, tiled=True)
    ffn_all = ffn_all.reshape(4, width, 3 * quarter)
    ffn_outs = [
        jnp.concatenate(
            [ffn_all[k, :, m * quarter : (m + 1) * quarter] for k in range(4)], axis=1
        )[:, :hidden].astype(WIDE)
        for m in range(3)
    ]

    attn_sum = add(attn_sum, swapped(attn_sum, "xl"))
    shared = attn_sum[split:]
    attn_sum = jnp.concatenate([attn_sum[:split], add(shared, swapped(shared, "tensor"))], axis=0)
    attn_sum = absolute(direct_gather(attn_sum, "z"), z, 0)
    other_sum = swapped(attn_sum, "core")
    attn_sum = jnp.stack(
        [
            jnp.where(first_core, attn_sum, other_sum),
            jnp.where(first_core, other_sum, attn_sum),
        ]
    ).astype(WIDE)
    own_sums = attn_sum[:, :, :split].reshape(2 * width, 512)
    shared_sums = attn_sum[:, :, split:].reshape(width + 32, 512)
    gain_sums = shared_sums[width:]

    return (
        output.astype(LOW)[None],
        grad_inputs[None],
        own_sums[:width],
        shared_sums[:width, :head_size],
        shared_sums[:width, head_size:],
        own_sums[width:].T,
        ffn_outs[0],
        ffn_outs[1],
        ffn_outs[2].T,
        gain_sums[0, :width],
        gain_sums[1, :width],
        gain_sums[4, : head_size // 4],
        gain_sums[4, head_size // 4 : head_size // 2],
        gain_sums[2, :width],
        gain_sums[3, :width],
    )


def solution(mesh):
    parts = Mesh(mesh.devices.reshape(4, 2, 2, 4, 2), ("z", "xl", "core", "ctx", "tensor"))
    rep = ("z", "xl", "core")
    return jax.shard_map(
        shards,
        mesh=parts,
        in_specs=(
            P(rep, "ctx", None),
            P(rep, None),
            P("ctx", "tensor"),
            P("ctx", None),
            P("ctx", None),
            P("tensor", "ctx"),
            P("ctx", "tensor"),
            P("ctx", "tensor"),
            P("tensor", "ctx"),
            P("ctx"),
            P("ctx"),
            P("ctx"),
            P("ctx"),
            P("ctx"),
            P("ctx"),
            P(rep, "ctx", None),
        ),
        out_specs=(
            P(rep, "ctx", None),
            P(rep, "ctx", None),
            P("ctx", "tensor"),
            P("ctx", None),
            P("ctx", None),
            P("tensor", "ctx"),
            P("ctx", "tensor"),
            P("ctx", "tensor"),
            P("tensor", "ctx"),
            P("ctx"),
            P("ctx"),
            P("ctx"),
            P("ctx"),
            P("ctx"),
            P("ctx"),
        ),
        check_vma=False,
    )
```

```python
import jax
import jax.numpy as jnp
from jax import lax
from jax.sharding import Mesh
from jax.sharding import PartitionSpec as P

WINDOW = 512
EPSILON = 1e-06
ROTARY_BASE = 10000.0
MASKED = -1e30
GELU = 0.7978845608028654
LOW = jnp.bfloat16
WIDE = jnp.float32

RING = [(i, (i + 1) % 4) for i in range(4)]
BACK = [(i, (i - 1) % 4) for i in range(4)]
ACROSS = [(i, (i + 2) % 4) for i in range(4)]
SWAP = [(0, 1), (1, 0)]


def send(x, axis, pairs):
    return lax.ppermute(x, axis, pairs)


def swapped(x, axis):
    return lax.ppermute(x, axis, SWAP)


def after(x, *others):
    return lax.optimization_barrier((x, *others))[0]


def direct_gather(x, axis):
    previous = send(x, axis, RING)
    following = send(x, axis, BACK)
    opposite = send(x, axis, ACROSS)
    return [x, following, opposite, previous]


def direct_terms(x, at, axis):
    own, following, opposite, previous = (
        lax.dynamic_index_in_dim(x, lax.rem(at + j, 4), 0, keepdims=False) for j in range(4)
    )
    return [
        own,
        send(following, axis, RING),
        send(previous, axis, BACK),
        send(opposite, axis, ACROSS),
    ]


def add(*terms):
    return sum(term.astype(WIDE) for term in terms).astype(LOW)


def absolute(blocks, at, dim):
    whole = jnp.zeros(
        blocks[0].shape[:dim] + (4,) + blocks[0].shape[dim:], blocks[0].dtype
    )
    for j, block in enumerate(blocks):
        whole = lax.dynamic_update_index_in_dim(whole, block, lax.rem(at + j, 4), dim)
    return whole


def rms_norm(values, gain):
    scale = lax.rsqrt(jnp.mean(values * values, axis=-1, keepdims=True) + EPSILON)
    return values * scale * gain


def rotate(values, cosine, sine):
    half = values.shape[-1] // 2
    first = values[..., :half]
    second = values[..., half:]
    return jnp.concatenate(
        [first * cosine - second * sine, second * cosine + first * sine], axis=-1
    )


def dot_plain(left, right):
    return jnp.dot(left, right, preferred_element_type=WIDE)


def dot_right(left, right):
    return lax.dot_general(left, right, (((1,), (1,)), ((), ())), preferred_element_type=WIDE)


def dot_left(left, right):
    return lax.dot_general(left, right, (((0,), (0,)), ((), ())), preferred_element_type=WIDE)


def with_core(x):
    return jnp.concatenate([x, swapped(x, "core")], axis=0)


def shards(
    tokens,
    doc_ids,
    w_query,
    w_key,
    w_value,
    w_out,
    w_gate,
    w_up,
    w_down,
    gain_in,
    gain_attn_out,
    gain_query,
    gain_key,
    gain_ffn_in,
    gain_ffn_out,
    cotangent,
):
    c = lax.axis_index("ctx")
    z = lax.axis_index("z")
    first_core = lax.axis_index("core") == 0
    width = w_query.shape[0]
    model = 4 * width
    head_size = w_key.shape[1]
    heads = w_query.shape[1] // head_size
    zrows = width // 4
    span = tokens.shape[1]

    hidden = w_gate.shape[1]
    share = (hidden // 2 + 127) // 128 * 128
    half_out = width // 2
    w_out_t = w_out.T
    w_kv = jnp.concatenate([w_key, w_value], axis=1)

    def gain_row(gain):
        return jnp.pad(gain, (0, 512 - gain.shape[-1]))[None]

    gain_rows = jnp.concatenate(
        [
            gain_row(gain)
            for gain in (gain_in, gain_attn_out, gain_ffn_in, gain_ffn_out, gain_query, gain_key)
        ]
        + [jnp.zeros((2, 512), LOW)],
        axis=0,
    )
    first_own = jnp.concatenate(
        [
            jnp.where(first_core, w_query, w_kv),
            jnp.where(first_core, w_out_t[:half_out], w_out_t[half_out:]),
            gain_rows,
        ],
        axis=0,
    )
    first_blocks = direct_gather(first_own, "ctx")

    def core_share(x):
        return jnp.where(
            first_core,
            x[:, :share],
            jnp.pad(x[:, share:], ((0, 0), (0, 2 * share - hidden))),
        )

    def z_rows(x):
        return lax.dynamic_slice_in_dim(x, z * zrows, zrows, axis=0)

    ffn_own = jnp.concatenate(
        [core_share(z_rows(x)) for x in (w_gate, w_up, w_down.T)], axis=1
    )
    full_ffn = lax.all_gather(ffn_own, ("ctx", "z"), axis=0, tiled=True)
    full_gate_up = full_ffn[:, : 2 * share]
    full_down_t = full_ffn[:, 2 * share :]

    swap_rows = width + half_out
    gain_table = jnp.concatenate([block[swap_rows:] for block in first_blocks], axis=0)

    def gain_lanes(row, rows, lanes):
        return jnp.concatenate(
            [
                lax.dynamic_slice(
                    gain_table, (8 * lax.rem(4 + k - c, 4) + row, 0), (rows, lanes)
                )
                for k in range(4)
            ],
            axis=1,
        ).astype(WIDE)

    norm_in, norm_attn, norm_ffn_in, norm_ffn_out = gain_lanes(0, 4, width)
    norm_query, norm_key = gain_lanes(4, 2, head_size // 4)
    mine = absolute([block[:swap_rows] for block in first_blocks], c, 0)
    theirs = swapped(mine, "core")
    low_half = jnp.where(first_core, mine, theirs)
    high_half = jnp.where(first_core, theirs, mine)
    full_query = low_half[:, :width].reshape(model, -1)
    full_kv = high_half[:, :width].reshape(model, -1)
    full_out_t = jnp.concatenate([low_half[:, width:], high_half[:, width:]], axis=1)
    full_out_t = full_out_t.reshape(model, -1)

    inputs = tokens[0].astype(WIDE)
    outward = cotangent[0].astype(WIDE)
    start = c * span
    doc_row = doc_ids[0]
    reach = 2 * span
    query_docs = lax.dynamic_slice_in_dim(doc_row, start, span)
    query_at = start + jnp.arange(span, dtype=jnp.int32)
    earlier = jnp.sum((doc_row[None, :] < query_docs[:, None]).astype(jnp.int32), axis=1)
    places = (query_at - earlier).astype(WIDE)
    half = head_size // 2
    freqs = ROTARY_BASE ** (-2.0 * jnp.arange(half, dtype=WIDE) / head_size)
    angles = places[:, None] * freqs[None, :]
    cosine = jnp.cos(angles)
    sine = jnp.sin(angles)
    padded_docs = jnp.concatenate([jnp.full((reach,), -1, jnp.int32), doc_row])
    key_docs = lax.dynamic_slice_in_dim(padded_docs, start, reach + span)
    key_at = start - reach + jnp.arange(reach + span, dtype=jnp.int32)
    allowed = (
        (query_docs[:, None] == key_docs[None, :])
        & (key_at[None, :] <= query_at[:, None])
        & (query_at[:, None] - key_at[None, :] < WINDOW)
    )

    cosine_rows = jnp.concatenate([cosine] * heads, axis=0)
    sine_rows = jnp.concatenate([sine] * heads, axis=0)
    allowed_rows = jnp.concatenate([allowed] * heads, axis=0)

    def stacked(x):
        return jnp.concatenate(
            [x[:, k * head_size : (k + 1) * head_size] for k in range(heads)], axis=0
        )

    def side_by_side(x):
        return jnp.concatenate([x[k * span : (k + 1) * span] for k in range(heads)], axis=1)

    def query_prep(raw, gain):
        return rotate(rms_norm(raw, gain), cosine_rows, sine_rows) * head_size ** (-0.5)

    def key_prep(raw, gain):
        return rotate(rms_norm(raw, gain), cosine, sine)

    normed_low = rms_norm(inputs, norm_in).astype(LOW)
    kv_raw = dot_plain(normed_low, full_kv)
    key_raw = kv_raw[:, :head_size]
    key_low = key_prep(key_raw, norm_key).astype(LOW)
    value_low = kv_raw[:, head_size:].astype(LOW)
    kv_low = jnp.concatenate([key_low, value_low], axis=1)
    before2 = send(kv_low, "ctx", [(0, 2), (1, 3)])
    before1 = send(kv_low, "ctx", [(0, 1), (1, 2), (2, 3)])
    query_raw = stacked(dot_plain(normed_low, full_query))
    query_low = query_prep(query_raw, norm_query).astype(LOW)
    all_kv = jnp.concatenate([before2, before1, kv_low], axis=0)
    all_keys = all_kv[:, :head_size]
    all_values = all_kv[:, head_size:]
    scores = jnp.where(allowed_rows, dot_right(query_low, all_keys), MASKED)
    largest = jnp.max(scores, axis=-1, keepdims=True)
    total_log = largest + jnp.log(jnp.sum(jnp.exp(scores - largest), axis=-1, keepdims=True))
    probs = jnp.exp(scores - total_log)
    probs_low = probs.astype(LOW)
    attended_low = side_by_side(dot_plain(probs_low, all_values)).astype(LOW)
    branch_mine = dot_right(attended_low, full_out_t).astype(LOW)
    branch_theirs = swapped(branch_mine, "tensor")
    branch = branch_mine.astype(WIDE) + branch_theirs.astype(WIDE)
    between = inputs + rms_norm(branch, norm_attn)

    ffn_in_low = rms_norm(between, norm_ffn_in).astype(LOW)
    ffn_rows = with_core(ffn_in_low)
    gate_up = dot_plain(ffn_rows, full_gate_up)
    gate = gate_up[:, :share]
    upward = gate_up[:, share:]
    bend = GELU * (1.0 + 0.134145 * gate * gate)
    level = jnp.tanh(GELU * gate * (1.0 + 0.044715 * gate * gate))
    gelu = 0.5 * gate * (1.0 + level)
    gelu_slope = 0.5 * (1.0 + level) + 0.5 * gate * (1.0 - level * level) * bend
    active_low, gelu_low, gate_factor = lax.optimization_barrier(
        (
            (gelu * upward).astype(LOW),
            gelu.astype(LOW),
            (upward * gelu_slope).astype(LOW),
        )
    )
    result_part = dot_right(active_low, full_down_t)
    result_given = result_part[span:].astype(LOW)
    result_mine = (
        result_part[:span] + swapped(result_given, "core").astype(WIDE)
    ).astype(LOW)
    result = result_mine.astype(WIDE) + swapped(result_mine, "tensor").astype(WIDE)
    unused, pull_out = jax.vjp(lambda v: rms_norm(v, norm_ffn_out), result)
    (grad_result,) = pull_out(outward)
    result_rows = with_core(grad_result.astype(LOW))
    grad_active = dot_plain(result_rows, full_down_t)
    gate_low, upward_low = lax.optimization_barrier(
        (
            (grad_active * gate_factor.astype(WIDE)).astype(LOW),
            (grad_active * gelu_low.astype(WIDE)).astype(LOW),
        )
    )
    both_low = jnp.concatenate([gate_low, upward_low], axis=1)
    ffn_grads = jnp.concatenate(
        [
            dot_left(ffn_rows, both_low).astype(LOW),
            dot_left(result_rows, active_low).astype(LOW),
        ],
        axis=1,
    )
    ffn_sum = lax.psum_scatter(ffn_grads, ("ctx", "z"), scatter_dimension=0, tiled=True)
    hidden_part = dot_right(after(both_low, ffn_grads), full_gate_up)
    hidden_given = hidden_part[span:].astype(LOW)
    hidden_mine = (
        hidden_part[:span] + swapped(hidden_given, "core").astype(WIDE)
    ).astype(LOW)
    hidden_theirs = swapped(hidden_mine, "tensor")
    grad_ffn_in = hidden_mine.astype(WIDE) + hidden_theirs.astype(WIDE)
    unused, pull_ffn_norm = jax.vjp(lambda v: rms_norm(v, norm_ffn_in), between)
    (grad_hidden_norm,) = pull_ffn_norm(grad_ffn_in)
    grad_hidden = outward + grad_hidden_norm

    unused, pull_attn_norm = jax.vjp(lambda v: rms_norm(v, norm_attn), branch)
    (grad_branch,) = pull_attn_norm(grad_hidden)
    branch_low = grad_branch.astype(LOW)
    grad_attended = stacked(dot_plain(branch_low, full_out_t).astype(LOW))
    grad_probs = dot_right(grad_attended, all_values)
    grad_scores = (
        probs * (grad_probs - jnp.sum(probs * grad_probs, axis=-1, keepdims=True))
    ).astype(LOW)
    grad_keys = dot_left(grad_scores, query_low)
    grad_values = dot_left(probs_low, grad_attended)
    grad_kv = jnp.concatenate([grad_keys, grad_values], axis=1)
    grad_kv_low = grad_kv[:reach].astype(LOW)
    back1 = send(grad_kv_low[span:], "ctx", [(1, 0), (2, 1), (3, 2)])
    back2 = send(grad_kv_low[:span], "ctx", [(2, 0), (3, 1)])
    grad_queries = dot_plain(grad_scores, all_keys)
    unused, pull_query = jax.vjp(lambda v: query_prep(v, norm_query), query_raw)
    (grad_query_raw,) = pull_query(grad_queries)
    query_grad_low = side_by_side(grad_query_raw).astype(LOW)
    own_kv = grad_kv[reach:] + back1.astype(WIDE) + back2.astype(WIDE)
    unused, pull_key = jax.vjp(lambda v: key_prep(v, norm_key), key_raw)
    (grad_key_raw,) = pull_key(own_kv[:, :head_size])
    kv_grad_low = jnp.concatenate([grad_key_raw, own_kv[:, head_size:]], axis=1).astype(LOW)
    normed_part = dot_right(query_grad_low, full_query) + dot_right(kv_grad_low, full_kv)
    normed_mine = normed_part.astype(LOW)
    normed_theirs = swapped(normed_mine, "tensor")

    own_terms = jnp.concatenate(
        [
            dot_left(normed_low, query_grad_low).astype(LOW).reshape(4, width, -1),
            dot_left(branch_low, attended_low).astype(LOW).reshape(4, width, -1),
        ],
        axis=1,
    )
    def unit(values):
        return values * lax.rsqrt(jnp.mean(values * values, axis=-1, keepdims=True) + EPSILON)

    def gain_grad(row, weight, values, grad):
        ones = jnp.where(jnp.arange(8)[:, None] == row, weight, 0.0)
        ones = jnp.broadcast_to(ones, (8, values.shape[0])).astype(LOW)
        return dot_plain(ones, (unit(values) * grad).astype(LOW))

    query_turned = rotate(grad_queries, cosine_rows, -sine_rows) * head_size ** (-0.5)
    key_turned = rotate(own_kv[:, :head_size], cosine, -sine)
    model_gains = (
        gain_grad(1, 0.5, branch, grad_hidden)
        + gain_grad(2, 0.5, between, grad_ffn_in)
        + gain_grad(3, 0.5, result, outward)
        + gain_grad(0, 1.0, inputs, normed_part)
    )
    head_gains = gain_grad(4, 1.0, query_raw, query_turned) + gain_grad(
        5, 1.0, key_raw, key_turned
    )

    def gain_block(x, k):
        lanes = x.shape[1] // 4
        return jnp.pad(x[:, k * lanes : (k + 1) * lanes], ((0, 24), (0, 512 - lanes)))

    gain_terms = jnp.stack(
        [gain_block(model_gains, k) + gain_block(head_gains, k) for k in range(4)]
    ).astype(LOW)
    shared_terms = jnp.concatenate(
        [
            dot_left(normed_low, kv_grad_low).astype(LOW).reshape(4, width, -1),
            gain_terms,
        ],
        axis=1,
    )
    terms = jnp.concatenate(
        [own_terms.reshape(4, 2, 4, -1, 512), shared_terms.reshape(4, 2, 4, -1, 512)], axis=3
    )
    split = own_terms.shape[1] // 8
    kept = jnp.where(first_core, terms[:, 0], terms[:, 1])
    given = jnp.where(first_core, terms[:, 1], terms[:, 0])
    attn_terms = add(kept, swapped(given, "core"))
    attn_own, *attn_moved = direct_terms(attn_terms, c, "ctx")

    quarter = share // 2
    first_x = lax.axis_index("xl") == 0

    def columns(x, side):
        return jnp.concatenate(
            [x[:, (2 * k + side) * quarter : (2 * k + side + 1) * quarter] for k in range(3)],
            axis=1,
        )

    *attn_moved, normed_theirs = lax.optimization_barrier((*attn_moved, normed_theirs))
    attn_sum = add(attn_own, *attn_moved)
    attn_own, *attn_moved = direct_terms(attn_sum, z, "z")
    ffn_sum = after(ffn_sum, *attn_moved)
    low_side = columns(ffn_sum, 0)
    high_side = columns(ffn_sum, 1)
    ffn_sum = add(
        jnp.where(first_x, low_side, high_side),
        swapped(jnp.where(first_x, high_side, low_side), "xl"),
    )
    ffn_all = lax.all_gather(ffn_sum, ("core", "xl", "z"), axis=0, tiled=True)
    ffn_all = ffn_all.reshape(4, width, 3 * quarter)
    ffn_outs = [
        jnp.concatenate(
            [ffn_all[k, :, m * quarter : (m + 1) * quarter] for k in range(4)], axis=1
        )[:, :hidden].astype(WIDE)
        for m in range(3)
    ]

    output = between + rms_norm(result, norm_ffn_out)
    grad_normed = normed_mine.astype(WIDE) + normed_theirs.astype(WIDE)
    unused, pull_in = jax.vjp(lambda v: rms_norm(v, norm_in), inputs)
    (grad_inputs_norm,) = pull_in(grad_normed)
    grad_inputs = grad_hidden + grad_inputs_norm

    attn_sum = add(attn_own, *attn_moved)
    shared = attn_sum[split:]
    across_x = swapped(attn_sum, "xl").astype(WIDE)
    across_both = send(shared, ("xl", "tensor"), [(0, 3), (1, 2), (2, 1), (3, 0)])
    shared_pair = shared.astype(WIDE) + swapped(shared, "tensor").astype(WIDE)
    other_pair = across_x[split:] + across_both.astype(WIDE)
    attn_sum = jnp.concatenate(
        [attn_sum[:split].astype(WIDE) + across_x[:split], shared_pair + other_pair], axis=0
    ).astype(LOW)
    attn_sum = absolute(direct_gather(attn_sum, "z"), z, 0)
    other_sum = after(swapped(attn_sum, "core"), *ffn_outs)
    attn_sum = jnp.stack(
        [
            jnp.where(first_core, attn_sum, other_sum),
            jnp.where(first_core, other_sum, attn_sum),
        ]
    ).astype(WIDE)
    own_sums = attn_sum[:, :, :split].reshape(2 * width, 512)
    shared_sums = attn_sum[:, :, split:].reshape(width + 32, 512)
    gain_sums = shared_sums[width:]

    return (
        output.astype(LOW)[None],
        grad_inputs[None],
        own_sums[:width],
        shared_sums[:width, :head_size],
        shared_sums[:width, head_size:],
        own_sums[width:].T,
        ffn_outs[0],
        ffn_outs[1],
        ffn_outs[2].T,
        gain_sums[0, :width],
        gain_sums[1, :width],
        gain_sums[4, : head_size // 4],
        gain_sums[5, : head_size // 4],
        gain_sums[2, :width],
        gain_sums[3, :width],
    )


def solution(mesh):
    parts = Mesh(mesh.devices.reshape(4, 2, 2, 4, 2), ("z", "xl", "core", "ctx", "tensor"))
    rep = ("z", "xl", "core")
    return jax.shard_map(
        shards,
        mesh=parts,
        in_specs=(
            P(rep, "ctx", None),
            P(rep, None),
            P("ctx", "tensor"),
            P("ctx", None),
            P("ctx", None),
            P("tensor", "ctx"),
            P("ctx", "tensor"),
            P("ctx", "tensor"),
            P("tensor", "ctx"),
            P("ctx"),
            P("ctx"),
            P("ctx"),
            P("ctx"),
            P("ctx"),
            P("ctx"),
            P(rep, "ctx", None),
        ),
        out_specs=(
            P(rep, "ctx", None),
            P(rep, "ctx", None),
            P("ctx", "tensor"),
            P("ctx", None),
            P("ctx", None),
            P("tensor", "ctx"),
            P("ctx", "tensor"),
            P("ctx", "tensor"),
            P("tensor", "ctx"),
            P("ctx"),
            P("ctx"),
            P("ctx"),
            P("ctx"),
            P("ctx"),
            P("ctx"),
        ),
        check_vma=False,
    )
```

```python
import jax
import jax.numpy as jnp
from jax import lax
from jax.sharding import Mesh
from jax.sharding import PartitionSpec as P

WINDOW = 512
EPSILON = 1e-06
ROTARY_BASE = 10000.0
MASKED = -1e30
GELU = 0.7978845608028654
LOW = jnp.bfloat16
WIDE = jnp.float32

RING = [(i, (i + 1) % 4) for i in range(4)]
BACK = [(i, (i - 1) % 4) for i in range(4)]
ACROSS = [(i, (i + 2) % 4) for i in range(4)]
SWAP = [(0, 1), (1, 0)]


def send(x, axis, pairs):
    return lax.ppermute(x, axis, pairs)


def swapped(x, axis):
    return lax.ppermute(x, axis, SWAP)


def after(x, *others):
    return lax.optimization_barrier((x, *others))[0]


def direct_gather(x, axis):
    previous = send(x, axis, RING)
    following = send(x, axis, BACK)
    opposite = send(x, axis, ACROSS)
    return [x, following, opposite, previous]


def ring_terms(x, at):
    return [
        lax.dynamic_index_in_dim(x, lax.rem(at + j, 4), 0, keepdims=False) for j in range(4)
    ]


def direct_terms(blocks, axis):
    own, following, opposite, previous = blocks
    return [
        own,
        send(following, axis, RING),
        send(previous, axis, BACK),
        send(opposite, axis, ACROSS),
    ]


def add(*terms):
    return sum(term.astype(WIDE) for term in terms).astype(LOW)


def absolute(blocks, at, dim):
    whole = jnp.zeros(
        blocks[0].shape[:dim] + (4,) + blocks[0].shape[dim:], blocks[0].dtype
    )
    for j, block in enumerate(blocks):
        whole = lax.dynamic_update_index_in_dim(whole, block, lax.rem(at + j, 4), dim)
    return whole


def rms_norm(values, gain):
    scale = lax.rsqrt(jnp.mean(values * values, axis=-1, keepdims=True) + EPSILON)
    return values * scale * gain


def rotate(values, cosine, sine):
    half = values.shape[-1] // 2
    first = values[..., :half]
    second = values[..., half:]
    return jnp.concatenate(
        [first * cosine - second * sine, second * cosine + first * sine], axis=-1
    )


def dot_plain(left, right):
    return jnp.dot(left, right, preferred_element_type=WIDE)


def dot_right(left, right):
    return lax.dot_general(left, right, (((1,), (1,)), ((), ())), preferred_element_type=WIDE)


def dot_left(left, right):
    return lax.dot_general(left, right, (((0,), (0,)), ((), ())), preferred_element_type=WIDE)


def with_core(x):
    return jnp.concatenate([x, swapped(x, "core")], axis=0)


def shards(
    tokens,
    doc_ids,
    w_query,
    w_key,
    w_value,
    w_out,
    w_gate,
    w_up,
    w_down,
    gain_in,
    gain_attn_out,
    gain_query,
    gain_key,
    gain_ffn_in,
    gain_ffn_out,
    cotangent,
):
    c = lax.axis_index("ctx")
    z = lax.axis_index("z")
    first_core = lax.axis_index("core") == 0
    width = w_query.shape[0]
    model = 4 * width
    head_size = w_key.shape[1]
    heads = w_query.shape[1] // head_size
    zrows = width // 4
    span = tokens.shape[1]

    hidden = w_gate.shape[1]
    share = (hidden // 2 + 127) // 128 * 128
    half_out = width // 2
    w_out_t = w_out.T
    w_kv = jnp.concatenate([w_key, w_value], axis=1)

    def gain_row(gain):
        return jnp.pad(gain, (0, 512 - gain.shape[-1]))[None]

    gain_rows = jnp.concatenate(
        [
            gain_row(gain)
            for gain in (gain_in, gain_attn_out, gain_ffn_in, gain_ffn_out, gain_query, gain_key)
        ]
        + [jnp.zeros((2, 512), LOW)],
        axis=0,
    )
    first_own = jnp.concatenate(
        [
            jnp.where(first_core, w_query, w_kv),
            jnp.where(first_core, w_out_t[:half_out], w_out_t[half_out:]),
            gain_rows,
        ],
        axis=0,
    )
    first_blocks = direct_gather(first_own, "ctx")

    def core_share(x):
        return jnp.where(
            first_core,
            x[:, :share],
            jnp.pad(x[:, share:], ((0, 0), (0, 2 * share - hidden))),
        )

    def z_rows(x):
        return lax.dynamic_slice_in_dim(x, z * zrows, zrows, axis=0)

    ffn_own = jnp.concatenate(
        [core_share(z_rows(x)) for x in (w_gate, w_up, w_down.T)], axis=1
    )
    full_ffn = lax.all_gather(ffn_own, ("ctx", "z"), axis=0, tiled=True)
    full_gate_up = full_ffn[:, : 2 * share]
    full_down_t = full_ffn[:, 2 * share :]

    swap_rows = width + half_out
    gain_table = jnp.concatenate([block[swap_rows:] for block in first_blocks], axis=0)

    def gain_lanes(row, rows, lanes):
        return jnp.concatenate(
            [
                lax.dynamic_slice(
                    gain_table, (8 * lax.rem(4 + k - c, 4) + row, 0), (rows, lanes)
                )
                for k in range(4)
            ],
            axis=1,
        ).astype(WIDE)

    norm_in, norm_attn, norm_ffn_in, norm_ffn_out = gain_lanes(0, 4, width)
    norm_query, norm_key = gain_lanes(4, 2, head_size // 4)
    mine = absolute([block[:swap_rows] for block in first_blocks], c, 0)
    theirs = swapped(mine, "core")
    low_half = jnp.where(first_core, mine, theirs)
    high_half = jnp.where(first_core, theirs, mine)
    full_query = low_half[:, :width].reshape(model, -1)
    full_kv = high_half[:, :width].reshape(model, -1)
    full_out_t = jnp.concatenate([low_half[:, width:], high_half[:, width:]], axis=1)
    full_out_t = full_out_t.reshape(model, -1)

    inputs = tokens[0].astype(WIDE)
    outward = cotangent[0].astype(WIDE)
    start = c * span
    doc_row = doc_ids[0]
    reach = 2 * span
    query_docs = lax.dynamic_slice_in_dim(doc_row, start, span)
    query_at = start + jnp.arange(span, dtype=jnp.int32)
    earlier = jnp.sum((doc_row[None, :] < query_docs[:, None]).astype(jnp.int32), axis=1)
    places = (query_at - earlier).astype(WIDE)
    half = head_size // 2
    freqs = ROTARY_BASE ** (-2.0 * jnp.arange(half, dtype=WIDE) / head_size)
    angles = places[:, None] * freqs[None, :]
    cosine = jnp.cos(angles)
    sine = jnp.sin(angles)
    padded_docs = jnp.concatenate([jnp.full((reach,), -1, jnp.int32), doc_row])
    key_docs = lax.dynamic_slice_in_dim(padded_docs, start, reach + span)
    key_at = start - reach + jnp.arange(reach + span, dtype=jnp.int32)
    allowed = (
        (query_docs[:, None] == key_docs[None, :])
        & (key_at[None, :] <= query_at[:, None])
        & (query_at[:, None] - key_at[None, :] < WINDOW)
    )

    cosine_rows = jnp.concatenate([cosine] * heads, axis=0)
    sine_rows = jnp.concatenate([sine] * heads, axis=0)
    allowed_rows = jnp.concatenate([allowed] * heads, axis=0)

    def stacked(x):
        return jnp.concatenate(
            [x[:, k * head_size : (k + 1) * head_size] for k in range(heads)], axis=0
        )

    def side_by_side(x):
        return jnp.concatenate([x[k * span : (k + 1) * span] for k in range(heads)], axis=1)

    def query_prep(raw, gain):
        return rotate(rms_norm(raw, gain), cosine_rows, sine_rows) * head_size ** (-0.5)

    def key_prep(raw, gain):
        return rotate(rms_norm(raw, gain), cosine, sine)

    normed_low = rms_norm(inputs, norm_in).astype(LOW)
    kv_raw = dot_plain(normed_low, full_kv)
    key_raw = kv_raw[:, :head_size]
    key_low = key_prep(key_raw, norm_key).astype(LOW)
    value_low = kv_raw[:, head_size:].astype(LOW)
    kv_low = jnp.concatenate([key_low, value_low], axis=1)
    before2 = send(kv_low, "ctx", [(0, 2), (1, 3)])
    before1 = send(kv_low, "ctx", [(0, 1), (1, 2), (2, 3)])
    query_raw = stacked(dot_plain(normed_low, full_query))
    query_low = query_prep(query_raw, norm_query).astype(LOW)
    all_kv = jnp.concatenate([before2, before1, kv_low], axis=0)
    all_keys = all_kv[:, :head_size]
    all_values = all_kv[:, head_size:]
    scores = jnp.where(allowed_rows, dot_right(query_low, all_keys), MASKED)
    largest = jnp.max(scores, axis=-1, keepdims=True)
    total_log = largest + jnp.log(jnp.sum(jnp.exp(scores - largest), axis=-1, keepdims=True))
    probs = jnp.exp(scores - total_log)
    probs_low = probs.astype(LOW)
    attended_low = side_by_side(dot_plain(probs_low, all_values)).astype(LOW)
    branch_mine = dot_right(attended_low, full_out_t).astype(LOW)
    branch_theirs = swapped(branch_mine, "tensor")
    branch = branch_mine.astype(WIDE) + branch_theirs.astype(WIDE)
    between = inputs + rms_norm(branch, norm_attn)

    ffn_in_low = rms_norm(between, norm_ffn_in).astype(LOW)
    ffn_rows = with_core(ffn_in_low)
    gate_up = dot_plain(ffn_rows, full_gate_up)
    gate = gate_up[:, :share]
    upward = gate_up[:, share:]
    bend = GELU * (1.0 + 0.134145 * gate * gate)
    level = jnp.tanh(GELU * gate * (1.0 + 0.044715 * gate * gate))
    gelu = 0.5 * gate * (1.0 + level)
    gelu_slope = 0.5 * (1.0 + level) + 0.5 * gate * (1.0 - level * level) * bend
    active_low, gelu_low, gate_factor = lax.optimization_barrier(
        (
            (gelu * upward).astype(LOW),
            gelu.astype(LOW),
            (upward * gelu_slope).astype(LOW),
        )
    )
    result_part = dot_right(active_low, full_down_t)
    result_given = result_part[span:].astype(LOW)
    result_mine = (
        result_part[:span] + swapped(result_given, "core").astype(WIDE)
    ).astype(LOW)
    result = result_mine.astype(WIDE) + swapped(result_mine, "tensor").astype(WIDE)
    unused, pull_out = jax.vjp(lambda v: rms_norm(v, norm_ffn_out), result)
    (grad_result,) = pull_out(outward)
    result_rows = with_core(grad_result.astype(LOW))
    grad_active = dot_plain(result_rows, full_down_t)
    gate_low, upward_low = lax.optimization_barrier(
        (
            (grad_active * gate_factor.astype(WIDE)).astype(LOW),
            (grad_active * gelu_low.astype(WIDE)).astype(LOW),
        )
    )
    both_low = jnp.concatenate([gate_low, upward_low], axis=1)
    ffn_grads = jnp.concatenate(
        [
            dot_left(ffn_rows, both_low).astype(LOW),
            dot_left(result_rows, active_low).astype(LOW),
        ],
        axis=1,
    )
    ffn_sum = lax.psum_scatter(ffn_grads, ("ctx", "z"), scatter_dimension=0, tiled=True)
    hidden_part = dot_right(after(both_low, ffn_grads), full_gate_up)
    hidden_given = hidden_part[span:].astype(LOW)
    hidden_mine = (
        hidden_part[:span] + swapped(hidden_given, "core").astype(WIDE)
    ).astype(LOW)
    hidden_theirs = swapped(hidden_mine, "tensor")
    grad_ffn_in = hidden_mine.astype(WIDE) + hidden_theirs.astype(WIDE)
    unused, pull_ffn_norm = jax.vjp(lambda v: rms_norm(v, norm_ffn_in), between)
    (grad_hidden_norm,) = pull_ffn_norm(grad_ffn_in)
    grad_hidden = outward + grad_hidden_norm

    unused, pull_attn_norm = jax.vjp(lambda v: rms_norm(v, norm_attn), branch)
    (grad_branch,) = pull_attn_norm(grad_hidden)
    branch_low = grad_branch.astype(LOW)
    grad_attended = stacked(dot_plain(branch_low, full_out_t).astype(LOW))
    grad_probs = dot_right(grad_attended, all_values)
    grad_scores = (
        probs * (grad_probs - jnp.sum(probs * grad_probs, axis=-1, keepdims=True))
    ).astype(LOW)
    grad_keys = dot_left(grad_scores, query_low)
    grad_values = dot_left(probs_low, grad_attended)
    grad_kv = jnp.concatenate([grad_keys, grad_values], axis=1)
    grad_kv_low = grad_kv[:reach].astype(LOW)
    back1 = send(grad_kv_low[span:], "ctx", [(1, 0), (2, 1), (3, 2)])
    back2 = send(grad_kv_low[:span], "ctx", [(2, 0), (3, 1)])
    grad_queries = dot_plain(grad_scores, all_keys)
    unused, pull_query = jax.vjp(lambda v: query_prep(v, norm_query), query_raw)
    (grad_query_raw,) = pull_query(grad_queries)
    query_grad_low = side_by_side(grad_query_raw).astype(LOW)
    own_kv = grad_kv[reach:] + back1.astype(WIDE) + back2.astype(WIDE)
    unused, pull_key = jax.vjp(lambda v: key_prep(v, norm_key), key_raw)
    (grad_key_raw,) = pull_key(own_kv[:, :head_size])
    kv_grad_low = jnp.concatenate([grad_key_raw, own_kv[:, head_size:]], axis=1).astype(LOW)
    normed_part = dot_right(query_grad_low, full_query) + dot_right(kv_grad_low, full_kv)
    normed_mine = normed_part.astype(LOW)
    normed_theirs = swapped(normed_mine, "tensor")

    own_terms = jnp.concatenate(
        [
            dot_left(normed_low, query_grad_low).astype(LOW).reshape(4, width, -1),
            dot_left(branch_low, attended_low).astype(LOW).reshape(4, width, -1),
        ],
        axis=1,
    )
    def unit(values):
        return values * lax.rsqrt(jnp.mean(values * values, axis=-1, keepdims=True) + EPSILON)

    def gain_grad(row, weight, values, grad):
        ones = jnp.where(jnp.arange(8)[:, None] == row, weight, 0.0)
        ones = jnp.broadcast_to(ones, (8, values.shape[0])).astype(LOW)
        return dot_plain(ones, (unit(values) * grad).astype(LOW))

    query_turned = rotate(grad_queries, cosine_rows, -sine_rows) * head_size ** (-0.5)
    key_turned = rotate(own_kv[:, :head_size], cosine, -sine)
    model_gains = (
        gain_grad(1, 0.5, branch, grad_hidden)
        + gain_grad(2, 0.5, between, grad_ffn_in)
        + gain_grad(3, 0.5, result, outward)
        + gain_grad(0, 1.0, inputs, normed_part)
    )
    head_gains = gain_grad(4, 1.0, query_raw, query_turned) + gain_grad(
        5, 1.0, key_raw, key_turned
    )

    def gain_block(x, k):
        lanes = x.shape[1] // 4
        return jnp.pad(x[:, k * lanes : (k + 1) * lanes], ((0, 24), (0, 512 - lanes)))

    gain_terms = jnp.stack(
        [gain_block(model_gains, k) + gain_block(head_gains, k) for k in range(4)]
    ).astype(LOW)
    shared_terms = jnp.concatenate(
        [
            dot_left(normed_low, kv_grad_low).astype(LOW).reshape(4, width, -1),
            gain_terms,
        ],
        axis=1,
    )
    terms = jnp.concatenate(
        [own_terms.reshape(4, 2, 4, -1, 512), shared_terms.reshape(4, 2, 4, -1, 512)], axis=3
    )
    split = own_terms.shape[1] // 8
    kept = jnp.where(first_core, terms[:, 0], terms[:, 1])
    given = jnp.where(first_core, terms[:, 1], terms[:, 0])
    attn_terms = add(kept, swapped(given, "core"))

    quarter = share // 2
    first_x = lax.axis_index("xl") == 0

    def columns(x, side):
        return jnp.concatenate(
            [x[:, (2 * k + side) * quarter : (2 * k + side + 1) * quarter] for k in range(3)],
            axis=1,
        )

    ffn_sum, normed_theirs, *attn_terms = lax.optimization_barrier(
        (ffn_sum, normed_theirs, *ring_terms(attn_terms, c))
    )
    attn_own, *attn_moved = direct_terms(attn_terms, "ctx")
    low_side = columns(ffn_sum, 0)
    high_side = columns(ffn_sum, 1)
    ffn_sum = add(
        jnp.where(first_x, low_side, high_side),
        swapped(jnp.where(first_x, high_side, low_side), "xl"),
    )
    ffn_all = lax.all_gather(ffn_sum, ("core", "xl", "z"), axis=0, tiled=True)
    ffn_all = ffn_all.reshape(4, width, 3 * quarter)
    ffn_outs = [
        ffn_all[:, :, m * quarter : (m + 1) * quarter]
        .transpose(1, 0, 2)
        .reshape(width, 4 * quarter)[:, :hidden]
        .astype(WIDE)
        for m in range(3)
    ]

    attn_sum = add(attn_own, *attn_moved)
    attn_own, *attn_moved = direct_terms(ring_terms(attn_sum, z), "z")

    output = between + rms_norm(result, norm_ffn_out)
    grad_normed = normed_mine.astype(WIDE) + normed_theirs.astype(WIDE)
    unused, pull_in = jax.vjp(lambda v: rms_norm(v, norm_in), inputs)
    (grad_inputs_norm,) = pull_in(grad_normed)
    grad_inputs = grad_hidden + grad_inputs_norm

    attn_sum = add(attn_own, *attn_moved)
    shared = attn_sum[split:]
    across_x = swapped(attn_sum, "xl").astype(WIDE)
    across_both = send(shared, ("xl", "tensor"), [(0, 3), (1, 2), (2, 1), (3, 0)])
    shared_pair = shared.astype(WIDE) + swapped(shared, "tensor").astype(WIDE)
    other_pair = across_x[split:] + across_both.astype(WIDE)
    attn_sum = jnp.concatenate(
        [attn_sum[:split].astype(WIDE) + across_x[:split], shared_pair + other_pair], axis=0
    ).astype(LOW)
    attn_blocks = direct_gather(attn_sum, "z")
    attn_blocks = lax.optimization_barrier((*attn_blocks, *ffn_outs))[:4]
    attn_sum = absolute(attn_blocks, z, 0)
    other_sum = swapped(attn_sum, "core")
    attn_sum = jnp.stack(
        [
            jnp.where(first_core, attn_sum, other_sum),
            jnp.where(first_core, other_sum, attn_sum),
        ]
    ).astype(WIDE)
    own_sums = attn_sum[:, :, :split].reshape(2 * width, 512)
    shared_sums = attn_sum[:, :, split:].reshape(width + 32, 512)
    gain_sums = shared_sums[width:]

    return (
        output.astype(LOW)[None],
        grad_inputs[None],
        own_sums[:width],
        shared_sums[:width, :head_size],
        shared_sums[:width, head_size:],
        own_sums[width:].T,
        ffn_outs[0],
        ffn_outs[1],
        ffn_outs[2].T,
        gain_sums[0, :width],
        gain_sums[1, :width],
        gain_sums[4, : head_size // 4],
        gain_sums[5, : head_size // 4],
        gain_sums[2, :width],
        gain_sums[3, :width],
    )


def solution(mesh):
    parts = Mesh(mesh.devices.reshape(4, 2, 2, 4, 2), ("z", "xl", "core", "ctx", "tensor"))
    rep = ("z", "xl", "core")
    return jax.shard_map(
        shards,
        mesh=parts,
        in_specs=(
            P(rep, "ctx", None),
            P(rep, None),
            P("ctx", "tensor"),
            P("ctx", None),
            P("ctx", None),
            P("tensor", "ctx"),
            P("ctx", "tensor"),
            P("ctx", "tensor"),
            P("tensor", "ctx"),
            P("ctx"),
            P("ctx"),
            P("ctx"),
            P("ctx"),
            P("ctx"),
            P("ctx"),
            P(rep, "ctx", None),
        ),
        out_specs=(
            P(rep, "ctx", None),
            P(rep, "ctx", None),
            P("ctx", "tensor"),
            P("ctx", None),
            P("ctx", None),
            P("tensor", "ctx"),
            P("ctx", "tensor"),
            P("ctx", "tensor"),
            P("tensor", "ctx"),
            P("ctx"),
            P("ctx"),
            P("ctx"),
            P("ctx"),
            P("ctx"),
            P("ctx"),
        ),
        check_vma=False,
    )
```

```python
import jax
import jax.numpy as jnp
from jax import lax
from jax.sharding import Mesh
from jax.sharding import PartitionSpec as P

WINDOW = 512
EPSILON = 1e-06
ROTARY_BASE = 10000.0
MASKED = -1e30
GELU = 0.7978845608028654
LOW = jnp.bfloat16
WIDE = jnp.float32

RING = [(i, (i + 1) % 4) for i in range(4)]
BACK = [(i, (i - 1) % 4) for i in range(4)]
ACROSS = [(i, (i + 2) % 4) for i in range(4)]
SWAP = [(0, 1), (1, 0)]


def send(x, axis, pairs):
    return lax.ppermute(x, axis, pairs)


def swapped(x, axis):
    return lax.ppermute(x, axis, SWAP)


def after(x, *others):
    return lax.optimization_barrier((x, *others))[0]


def direct_gather(x, axis):
    previous = send(x, axis, RING)
    following = send(x, axis, BACK)
    opposite = send(x, axis, ACROSS)
    return [x, following, opposite, previous]


def ring_gather(x, axis):
    h = x.shape[0] // 16 * 8
    previous = send(x, axis, RING)
    following = send(x, axis, BACK)
    opposite = jnp.concatenate(
        [send(previous[:h], axis, RING), send(following[h:], axis, BACK)], axis=0
    )
    return [x, following, opposite, previous]


def ring_terms(x, at):
    return [
        lax.dynamic_index_in_dim(x, lax.rem(at + j, 4), 0, keepdims=False) for j in range(4)
    ]


def direct_terms(blocks, axis):
    own, following, opposite, previous = blocks
    return [
        own,
        send(following, axis, RING),
        send(previous, axis, BACK),
        send(opposite, axis, ACROSS),
    ]


def add(*terms):
    return sum(term.astype(WIDE) for term in terms).astype(LOW)


def absolute(blocks, at, dim):
    whole = jnp.zeros(
        blocks[0].shape[:dim] + (4,) + blocks[0].shape[dim:], blocks[0].dtype
    )
    for j, block in enumerate(blocks):
        whole = lax.dynamic_update_index_in_dim(whole, block, lax.rem(at + j, 4), dim)
    return whole


def rms_norm(values, gain):
    scale = lax.rsqrt(jnp.mean(values * values, axis=-1, keepdims=True) + EPSILON)
    return values * scale * gain


def rotate(values, cosine, sine):
    half = values.shape[-1] // 2
    first = values[..., :half]
    second = values[..., half:]
    return jnp.concatenate(
        [first * cosine - second * sine, second * cosine + first * sine], axis=-1
    )


def dot_plain(left, right):
    return jnp.dot(left, right, preferred_element_type=WIDE)


def dot_right(left, right):
    return lax.dot_general(left, right, (((1,), (1,)), ((), ())), preferred_element_type=WIDE)


def dot_left(left, right):
    return lax.dot_general(left, right, (((0,), (0,)), ((), ())), preferred_element_type=WIDE)


def with_core(x):
    return jnp.concatenate([x, swapped(x, "core")], axis=0)


def shards(
    tokens,
    doc_ids,
    w_query,
    w_key,
    w_value,
    w_out,
    w_gate,
    w_up,
    w_down,
    gain_in,
    gain_attn_out,
    gain_query,
    gain_key,
    gain_ffn_in,
    gain_ffn_out,
    cotangent,
):
    c = lax.axis_index("ctx")
    z = lax.axis_index("z")
    first_core = lax.axis_index("core") == 0
    width = w_query.shape[0]
    model = 4 * width
    head_size = w_key.shape[1]
    heads = w_query.shape[1] // head_size
    zrows = width // 4
    span = tokens.shape[1]

    hidden = w_gate.shape[1]
    share = (hidden // 2 + 127) // 128 * 128
    half_out = width // 2
    w_out_t = w_out.T
    w_kv = jnp.concatenate([w_key, w_value], axis=1)

    def gain_row(gain):
        return jnp.pad(gain, (0, 512 - gain.shape[-1]))[None]

    gain_rows = jnp.concatenate(
        [
            gain_row(gain)
            for gain in (gain_in, gain_attn_out, gain_ffn_in, gain_ffn_out, gain_query, gain_key)
        ]
        + [jnp.zeros((2, 512), LOW)],
        axis=0,
    )
    first_own = jnp.concatenate(
        [
            jnp.where(first_core, w_query, w_kv),
            jnp.where(first_core, w_out_t[:half_out], w_out_t[half_out:]),
            gain_rows,
        ],
        axis=0,
    )
    first_blocks = ring_gather(first_own, "ctx")

    def core_share(x):
        return jnp.where(
            first_core,
            x[:, :share],
            jnp.pad(x[:, share:], ((0, 0), (0, 2 * share - hidden))),
        )

    def z_rows(x):
        return lax.dynamic_slice_in_dim(x, z * zrows, zrows, axis=0)

    ffn_own = jnp.concatenate(
        [core_share(z_rows(x)) for x in (w_gate, w_up, w_down.T)], axis=1
    )
    full_ffn = lax.all_gather(ffn_own, ("ctx", "z"), axis=0, tiled=True)
    full_gate_up = full_ffn[:, : 2 * share]
    full_down_t = full_ffn[:, 2 * share :]

    swap_rows = width + half_out
    gain_table = jnp.concatenate([block[swap_rows:] for block in first_blocks], axis=0)

    def gain_lanes(row, rows, lanes):
        return jnp.concatenate(
            [
                lax.dynamic_slice(
                    gain_table, (8 * lax.rem(4 + k - c, 4) + row, 0), (rows, lanes)
                )
                for k in range(4)
            ],
            axis=1,
        ).astype(WIDE)

    norm_in, norm_attn, norm_ffn_in, norm_ffn_out = gain_lanes(0, 4, width)
    norm_query, norm_key = gain_lanes(4, 2, head_size // 4)
    mine = absolute([block[:swap_rows] for block in first_blocks], c, 0)
    theirs = swapped(mine, "core")
    low_half = jnp.where(first_core, mine, theirs)
    high_half = jnp.where(first_core, theirs, mine)
    full_query = low_half[:, :width].reshape(model, -1)
    full_kv = high_half[:, :width].reshape(model, -1)
    full_out_t = jnp.concatenate([low_half[:, width:], high_half[:, width:]], axis=1)
    full_out_t = full_out_t.reshape(model, -1)

    inputs = tokens[0].astype(WIDE)
    outward = cotangent[0].astype(WIDE)
    start = c * span
    doc_row = doc_ids[0]
    reach = 2 * span
    query_docs = lax.dynamic_slice_in_dim(doc_row, start, span)
    query_at = start + jnp.arange(span, dtype=jnp.int32)
    earlier = jnp.sum((doc_row[None, :] < query_docs[:, None]).astype(jnp.int32), axis=1)
    places = (query_at - earlier).astype(WIDE)
    half = head_size // 2
    freqs = ROTARY_BASE ** (-2.0 * jnp.arange(half, dtype=WIDE) / head_size)
    angles = places[:, None] * freqs[None, :]
    cosine = jnp.cos(angles)
    sine = jnp.sin(angles)
    padded_docs = jnp.concatenate([jnp.full((reach,), -1, jnp.int32), doc_row])
    key_docs = lax.dynamic_slice_in_dim(padded_docs, start, reach + span)
    key_at = start - reach + jnp.arange(reach + span, dtype=jnp.int32)
    allowed = (
        (query_docs[:, None] == key_docs[None, :])
        & (key_at[None, :] <= query_at[:, None])
        & (query_at[:, None] - key_at[None, :] < WINDOW)
    )

    cosine_rows = jnp.concatenate([cosine] * heads, axis=0)
    sine_rows = jnp.concatenate([sine] * heads, axis=0)
    allowed_rows = jnp.concatenate([allowed] * heads, axis=0)

    def stacked(x):
        return jnp.concatenate(
            [x[:, k * head_size : (k + 1) * head_size] for k in range(heads)], axis=0
        )

    def side_by_side(x):
        return jnp.concatenate([x[k * span : (k + 1) * span] for k in range(heads)], axis=1)

    def query_prep(raw, gain):
        return rotate(rms_norm(raw, gain), cosine_rows, sine_rows) * head_size ** (-0.5)

    def key_prep(raw, gain):
        return rotate(rms_norm(raw, gain), cosine, sine)

    normed_low = rms_norm(inputs, norm_in).astype(LOW)
    kv_raw = dot_plain(normed_low, full_kv)
    key_raw = kv_raw[:, :head_size]
    key_low = key_prep(key_raw, norm_key).astype(LOW)
    value_low = kv_raw[:, head_size:].astype(LOW)
    kv_low = jnp.concatenate([key_low, value_low], axis=1)
    before2 = send(kv_low, "ctx", [(0, 2), (1, 3)])
    before1 = send(kv_low, "ctx", [(0, 1), (1, 2), (2, 3)])
    query_raw = stacked(dot_plain(normed_low, full_query))
    query_low = query_prep(query_raw, norm_query).astype(LOW)
    all_kv = jnp.concatenate([before2, before1, kv_low], axis=0)
    all_keys = all_kv[:, :head_size]
    all_values = all_kv[:, head_size:]
    scores = jnp.where(allowed_rows, dot_right(query_low, all_keys), MASKED)
    largest = jnp.max(scores, axis=-1, keepdims=True)
    total_log = largest + jnp.log(jnp.sum(jnp.exp(scores - largest), axis=-1, keepdims=True))
    probs = jnp.exp(scores - total_log)
    probs_low = probs.astype(LOW)
    attended_low = side_by_side(dot_plain(probs_low, all_values)).astype(LOW)
    branch_mine = dot_right(attended_low, full_out_t).astype(LOW)
    branch_theirs = swapped(branch_mine, "tensor")
    branch = branch_mine.astype(WIDE) + branch_theirs.astype(WIDE)
    between = inputs + rms_norm(branch, norm_attn)

    ffn_in_low = rms_norm(between, norm_ffn_in).astype(LOW)
    ffn_rows = with_core(ffn_in_low)
    gate_up = dot_plain(ffn_rows, full_gate_up)
    gate = gate_up[:, :share]
    upward = gate_up[:, share:]
    bend = GELU * (1.0 + 0.134145 * gate * gate)
    level = jnp.tanh(GELU * gate * (1.0 + 0.044715 * gate * gate))
    gelu = 0.5 * gate * (1.0 + level)
    gelu_slope = 0.5 * (1.0 + level) + 0.5 * gate * (1.0 - level * level) * bend
    active_low, gelu_low, gate_factor = lax.optimization_barrier(
        (
            (gelu * upward).astype(LOW),
            gelu.astype(LOW),
            (upward * gelu_slope).astype(LOW),
        )
    )
    result_part = dot_right(active_low, full_down_t)
    result_given = result_part[span:].astype(LOW)
    result_mine = (
        result_part[:span] + swapped(result_given, "core").astype(WIDE)
    ).astype(LOW)
    result = result_mine.astype(WIDE) + swapped(result_mine, "tensor").astype(WIDE)
    unused, pull_out = jax.vjp(lambda v: rms_norm(v, norm_ffn_out), result)
    (grad_result,) = pull_out(outward)
    result_rows = with_core(grad_result.astype(LOW))
    grad_active = dot_plain(result_rows, full_down_t)
    gate_low, upward_low = lax.optimization_barrier(
        (
            (grad_active * gate_factor.astype(WIDE)).astype(LOW),
            (grad_active * gelu_low.astype(WIDE)).astype(LOW),
        )
    )
    both_low = jnp.concatenate([gate_low, upward_low], axis=1)
    ffn_grads = jnp.concatenate(
        [
            dot_left(ffn_rows, both_low).astype(LOW),
            dot_left(result_rows, active_low).astype(LOW),
        ],
        axis=1,
    )
    ffn_sum = lax.psum_scatter(ffn_grads, ("ctx", "z"), scatter_dimension=0, tiled=True)
    hidden_part = dot_right(after(both_low, ffn_grads), full_gate_up)
    hidden_given = hidden_part[span:].astype(LOW)
    hidden_mine = (
        hidden_part[:span] + swapped(hidden_given, "core").astype(WIDE)
    ).astype(LOW)
    hidden_theirs = swapped(hidden_mine, "tensor")
    grad_ffn_in = hidden_mine.astype(WIDE) + hidden_theirs.astype(WIDE)
    unused, pull_ffn_norm = jax.vjp(lambda v: rms_norm(v, norm_ffn_in), between)
    (grad_hidden_norm,) = pull_ffn_norm(grad_ffn_in)
    grad_hidden = outward + grad_hidden_norm

    unused, pull_attn_norm = jax.vjp(lambda v: rms_norm(v, norm_attn), branch)
    (grad_branch,) = pull_attn_norm(grad_hidden)
    branch_low = grad_branch.astype(LOW)
    grad_attended = stacked(dot_plain(branch_low, full_out_t).astype(LOW))
    grad_probs = dot_right(grad_attended, all_values)
    grad_scores = (
        probs * (grad_probs - jnp.sum(probs * grad_probs, axis=-1, keepdims=True))
    ).astype(LOW)
    grad_keys = dot_left(grad_scores, query_low)
    grad_values = dot_left(probs_low, grad_attended)
    grad_kv = jnp.concatenate([grad_keys, grad_values], axis=1)
    grad_kv_low = grad_kv[:reach].astype(LOW)
    back1 = send(grad_kv_low[span:], "ctx", [(1, 0), (2, 1), (3, 2)])
    back2 = send(grad_kv_low[:span], "ctx", [(2, 0), (3, 1)])
    grad_queries = dot_plain(grad_scores, all_keys)
    unused, pull_query = jax.vjp(lambda v: query_prep(v, norm_query), query_raw)
    (grad_query_raw,) = pull_query(grad_queries)
    query_grad_low = side_by_side(grad_query_raw).astype(LOW)
    own_kv = grad_kv[reach:] + back1.astype(WIDE) + back2.astype(WIDE)
    unused, pull_key = jax.vjp(lambda v: key_prep(v, norm_key), key_raw)
    (grad_key_raw,) = pull_key(own_kv[:, :head_size])
    kv_grad_low = jnp.concatenate([grad_key_raw, own_kv[:, head_size:]], axis=1).astype(LOW)
    normed_part = dot_right(query_grad_low, full_query) + dot_right(kv_grad_low, full_kv)
    normed_mine = normed_part.astype(LOW)
    normed_theirs = swapped(normed_mine, "tensor")

    own_terms = jnp.concatenate(
        [
            dot_left(normed_low, query_grad_low).astype(LOW).reshape(4, width, -1),
            dot_left(branch_low, attended_low).astype(LOW).reshape(4, width, -1),
        ],
        axis=1,
    )
    def unit(values):
        return values * lax.rsqrt(jnp.mean(values * values, axis=-1, keepdims=True) + EPSILON)

    def gain_grad(row, weight, values, grad):
        ones = jnp.where(jnp.arange(8)[:, None] == row, weight, 0.0)
        ones = jnp.broadcast_to(ones, (8, values.shape[0])).astype(LOW)
        return dot_plain(ones, (unit(values) * grad).astype(LOW))

    query_turned = rotate(grad_queries, cosine_rows, -sine_rows) * head_size ** (-0.5)
    key_turned = rotate(own_kv[:, :head_size], cosine, -sine)
    model_gains = (
        gain_grad(1, 0.5, branch, grad_hidden)
        + gain_grad(2, 0.5, between, grad_ffn_in)
        + gain_grad(3, 0.5, result, outward)
        + gain_grad(0, 1.0, inputs, normed_part)
    )
    head_gains = gain_grad(4, 1.0, query_raw, query_turned) + gain_grad(
        5, 1.0, key_raw, key_turned
    )

    def gain_block(x, k):
        lanes = x.shape[1] // 4
        return jnp.pad(x[:, k * lanes : (k + 1) * lanes], ((0, 24), (0, 512 - lanes)))

    gain_terms = jnp.stack(
        [gain_block(model_gains, k) + gain_block(head_gains, k) for k in range(4)]
    ).astype(LOW)
    shared_terms = jnp.concatenate(
        [
            dot_left(normed_low, kv_grad_low).astype(LOW).reshape(4, width, -1),
            gain_terms,
        ],
        axis=1,
    )
    terms = jnp.concatenate(
        [own_terms.reshape(4, 2, 4, -1, 512), shared_terms.reshape(4, 2, 4, -1, 512)], axis=3
    )
    split = own_terms.shape[1] // 8
    kept = jnp.where(first_core, terms[:, 0], terms[:, 1])
    given = jnp.where(first_core, terms[:, 1], terms[:, 0])
    attn_terms = add(kept, swapped(given, "core"))

    quarter = share // 2
    first_x = lax.axis_index("xl") == 0

    def columns(x, side):
        return jnp.concatenate(
            [x[:, (2 * k + side) * quarter : (2 * k + side + 1) * quarter] for k in range(3)],
            axis=1,
        )

    ffn_sum, normed_theirs, *attn_terms = lax.optimization_barrier(
        (ffn_sum, normed_theirs, *ring_terms(attn_terms, c))
    )
    attn_own, *attn_moved = direct_terms(attn_terms, "ctx")
    low_side = columns(ffn_sum, 0)
    high_side = columns(ffn_sum, 1)
    ffn_sum = add(
        jnp.where(first_x, low_side, high_side),
        swapped(jnp.where(first_x, high_side, low_side), "xl"),
    )
    ffn_all = lax.all_gather(ffn_sum, ("core", "xl", "z"), axis=0, tiled=True)
    ffn_all = ffn_all.reshape(4, width, 3 * quarter)
    ffn_outs = [
        ffn_all[:, :, m * quarter : (m + 1) * quarter]
        .transpose(1, 0, 2)
        .reshape(width, 4 * quarter)[:, :hidden]
        .astype(WIDE)
        for m in range(3)
    ]

    attn_sum = add(attn_own, *attn_moved)
    attn_own, *attn_moved = direct_terms(ring_terms(attn_sum, z), "z")

    output = between + rms_norm(result, norm_ffn_out)
    grad_normed = normed_mine.astype(WIDE) + normed_theirs.astype(WIDE)
    unused, pull_in = jax.vjp(lambda v: rms_norm(v, norm_in), inputs)
    (grad_inputs_norm,) = pull_in(grad_normed)
    grad_inputs = grad_hidden + grad_inputs_norm

    attn_sum = add(attn_own, *attn_moved)
    shared = attn_sum[split:]
    across_x = swapped(attn_sum, "xl").astype(WIDE)
    across_both = send(shared, ("xl", "tensor"), [(0, 3), (1, 2), (2, 1), (3, 0)])
    shared_pair = shared.astype(WIDE) + swapped(shared, "tensor").astype(WIDE)
    other_pair = across_x[split:] + across_both.astype(WIDE)
    attn_sum = jnp.concatenate(
        [attn_sum[:split].astype(WIDE) + across_x[:split], shared_pair + other_pair], axis=0
    ).astype(LOW)
    attn_blocks = direct_gather(attn_sum, "z")
    attn_blocks = lax.optimization_barrier((*attn_blocks, *ffn_outs))[:4]
    attn_sum = absolute(attn_blocks, z, 0)
    other_sum = swapped(attn_sum, "core")
    attn_sum = jnp.stack(
        [
            jnp.where(first_core, attn_sum, other_sum),
            jnp.where(first_core, other_sum, attn_sum),
        ]
    ).astype(WIDE)
    own_sums = attn_sum[:, :, :split].reshape(2 * width, 512)
    shared_sums = attn_sum[:, :, split:].reshape(width + 32, 512)
    gain_sums = shared_sums[width:]

    return (
        output.astype(LOW)[None],
        grad_inputs[None],
        own_sums[:width],
        shared_sums[:width, :head_size],
        shared_sums[:width, head_size:],
        own_sums[width:].T,
        ffn_outs[0],
        ffn_outs[1],
        ffn_outs[2].T,
        gain_sums[0, :width],
        gain_sums[1, :width],
        gain_sums[4, : head_size // 4],
        gain_sums[5, : head_size // 4],
        gain_sums[2, :width],
        gain_sums[3, :width],
    )


def solution(mesh):
    parts = Mesh(mesh.devices.reshape(4, 2, 2, 4, 2), ("z", "xl", "core", "ctx", "tensor"))
    rep = ("z", "xl", "core")
    return jax.shard_map(
        shards,
        mesh=parts,
        in_specs=(
            P(rep, "ctx", None),
            P(rep, None),
            P("ctx", "tensor"),
            P("ctx", None),
            P("ctx", None),
            P("tensor", "ctx"),
            P("ctx", "tensor"),
            P("ctx", "tensor"),
            P("tensor", "ctx"),
            P("ctx"),
            P("ctx"),
            P("ctx"),
            P("ctx"),
            P("ctx"),
            P("ctx"),
            P(rep, "ctx", None),
        ),
        out_specs=(
            P(rep, "ctx", None),
            P(rep, "ctx", None),
            P("ctx", "tensor"),
            P("ctx", None),
            P("ctx", None),
            P("tensor", "ctx"),
            P("ctx", "tensor"),
            P("ctx", "tensor"),
            P("tensor", "ctx"),
            P("ctx"),
            P("ctx"),
            P("ctx"),
            P("ctx"),
            P("ctx"),
            P("ctx"),
        ),
        check_vma=False,
    )
```
